512 devices in a mesh: gx: 128 (over z, y, core), gy: 4 (over x).
Axes of the slice: x: 4, y: 8, z: 8, core: 2. Of those that a mesh axis runs over, the one named last changes fastest.
Arguments:
- jitter: float32 [3, 1024, 32, 128], P(None, 'gx', 'gy'), may hold values from -0.3 to 0.3
- colour: float32 [1024, 32, 128], P('gx', 'gy'), may hold values from 0 to 1
- surface_cells: int32 [128, 4, 192], P('gx', 'gy'), may hold values from 0 to 8191, as said below
- neighbours: int32 [128, 4, 192, 128], P('gx', 'gy'), may hold values from 0 to 342, as said below
- counts: int32 [128, 4], P('gx', 'gy'), may hold values from 1 to 192, as said below
- pressure: float32 [1024, 32, 128], P('gx', 'gy'), may hold values from -6 to 6
- source: float32 [1024, 32, 128], P('gx', 'gy'), may hold values from -6 to 6
Outputs:
- pressure_out: float32 [1024, 32, 128], P('gx', 'gy')
- curvature_out: float32 [128, 4, 192], P('gx', 'gy')
The draws below stay inside these ranges and needn't reach their ends.
Inputs may be any that keep to these rules, and one draw needn't show every extreme that they name: `surface_cells`: the cells of one tile's list are distinct. `neighbours`: each code names a step of -3 to 3 lattice cells along every dimension. Among the tiles that share a gx index the counts sum to exactly 256, and one of them has 192.
All inputs are finite; a program needn't handle non-finite values.
Results may differ from the reference program's by a relative error of at most 0.0003.
Values sent between devices are 32-bit elements; how exact they have to be, the bound alone decides.
No kernel may reach another device: no remote copies, remote signals or barrier semaphores. Data moves between devices by JAX's collectives and lax.ppermute only.
A program may use at most 64 MiB of HBM per device.

```python
import jax
import jax.numpy as jnp
from jax import lax

CX = 8
CY = 8
CZ = 128
SMEAN = 64
NB = 128
SWEEPS = 3
SMAX = 192
CELLS = 8192
NX = 1024
NY = 32
N_GX = 128
N_GY = 4


def surface_layout(key):
    tile_keys = jax.random.split(jax.random.fold_in(key, 11), N_GX * N_GY)
    orders = jax.vmap(lambda single: jax.random.permutation(single, CX * CY * CZ))(tile_keys)
    return orders[:, :SMAX].astype(jnp.int32).reshape(N_GX, N_GY, SMAX)


def draw_surface_cells(key, part):
    return surface_layout(key)


def draw_neighbours(key, part):
    codes = jax.random.randint(jax.random.fold_in(key, 23), (N_GX, N_GY, SMAX, NB), 0, 343)
    return codes.astype(jnp.int32)


def draw_counts(key, part):
    heavy = jax.random.randint(jax.random.fold_in(key, 31), (N_GX, 1), 0, N_GY)
    remain = (N_GY - 3) * SMEAN
    base = remain // (N_GY - 1)
    extra = remain - base * (N_GY - 1)
    swing = jax.random.randint(jax.random.fold_in(key, 37), (N_GX, N_GY - 1), 0, base // 2 + 1)
    order = jnp.arange(N_GY - 1)[None, :]
    others = base + (order < extra).astype(jnp.int32) + swing - jnp.roll(swing, 1, axis=1)
    places = jnp.arange(N_GY)[None, :]
    picked = jnp.clip(places - (places > heavy).astype(jnp.int32), 0, N_GY - 2)
    spread = jnp.take_along_axis(others, jnp.broadcast_to(picked, (N_GX, N_GY)), axis=1)
    return jnp.where(places == heavy, 3 * SMEAN, spread).astype(jnp.int32)


def level_of(key, dims, cuts, smallest, high):
    gain, own = 1.0, jax.random.fold_in(key, 6)
    for axis_at, parts in cuts:
        steps = jnp.exp(jax.random.uniform(jax.random.fold_in(own, axis_at), (parts,), jnp.float32, smallest / len(cuts), high / len(cuts)))
        gain = gain * jnp.repeat(steps, dims[axis_at] // parts).reshape([-1 if axis == axis_at else 1 for axis in range(len(dims))])
    return gain


def normal_values(key, dims, scale, most, cuts=(), held_as=jnp.bfloat16):
    result = jax.random.normal(key, dims, jnp.float32) * scale
    if len(cuts) > 0:
        result = level_of(key, dims, cuts, -0.22, 0.18) * result
    return jnp.clip(result, min=-most, max=most).astype(held_as)


def setup_inputs(seed: int = 0) -> dict:
    key_of = jax.random.split(jax.random.key(seed), 8)
    return {
        "jitter": jnp.clip(jax.random.uniform(key_of[0], (3, NX, NY, CZ), jnp.float32, -0.3, 0.3) * level_of(key_of[0], (3, NX, NY, CZ), ((1, 128), (2, 4)), -0.4, 0.0), -0.3, 0.3),
        "colour": jnp.clip(1.0 * jax.random.uniform(key_of[1], (NX, NY, CZ), jnp.float32) ** level_of(key_of[1], (NX, NY, CZ), ((0, 128), (1, 4)), -0.2, 0.2), 0.0, 1.0),
        "surface_cells": draw_surface_cells(jax.random.fold_in(key_of[7], 71), 0),
        "neighbours": draw_neighbours(jax.random.fold_in(key_of[7], 71), 0),
        "counts": draw_counts(jax.random.fold_in(key_of[7], 71), 0),
        "pressure": normal_values(key_of[5], (NX, NY, CZ), 1.0, 6.0, ((0, 128), (1, 4)), jnp.float32),
        "source": normal_values(key_of[6], (NX, NY, CZ), 1.0, 6.0, ((0, 128), (1, 4)), jnp.float32),
    }


SIGMA = 1.0
SMOOTH_SQ = 4.0

def lattice(size_x, size_y, size_z):
    indices = jnp.arange(size_x * size_y * size_z, dtype=jnp.int32)
    coord_x = (indices // (size_y * size_z)).astype(jnp.float32)
    coord_y = (indices // size_z % size_y).astype(jnp.float32)
    coord_z = (indices % size_z).astype(jnp.float32)
    return jnp.stack([coord_x, coord_y, coord_z])

def decode(cells, codes, size_x, size_y, size_z):
    base_x = (cells // (size_y * size_z))[:, None]
    base_y = (cells // size_z % size_y)[:, None]
    base_z = (cells % size_z)[:, None]
    near_x = jnp.clip(base_x + codes // 49 - 3, 0, size_x - 1)
    near_y = jnp.clip(base_y + codes // 7 % 7 - 3, 0, size_y - 1)
    near_z = jnp.clip(base_z + codes % 7 - 3, 0, size_z - 1)
    return ((near_x * size_y + near_y) * size_z + near_z).astype(jnp.int32)

def owner_rows(jitter_tile, colour_tile, cells, codes, count):
    neighbours = decode(cells, codes, CX, CY, CZ)
    places = lattice(CX, CY, CZ) + jitter_tile
    centre = places[:, cells]
    beside_all = places[:, neighbours]
    offsets = beside_all - centre[:, :, None]
    shade = colour_tile[neighbours] - colour_tile[cells][:, None]
    stacked = jnp.stack([offsets[0], offsets[1], offsets[2], shade], axis=1)
    live = jnp.arange(cells.shape[0], dtype=jnp.int32) < count
    return jnp.where(live[:, None, None], stacked, jnp.zeros_like(stacked))

def curvature(stacked):
    off_x = stacked[:, 0]
    off_y = stacked[:, 1]
    off_z = stacked[:, 2]
    shade = stacked[:, 3]
    weight = shade * jnp.exp(-(off_x * off_x + off_y * off_y + off_z * off_z) / SMOOTH_SQ)
    first = -2.0 / SMOOTH_SQ
    second = 4.0 / (SMOOTH_SQ * SMOOTH_SQ)
    grad_x = first * lax.optimization_barrier(jnp.sum(weight * off_x, axis=1))
    grad_y = first * lax.optimization_barrier(jnp.sum(weight * off_y, axis=1))
    grad_z = first * lax.optimization_barrier(jnp.sum(weight * off_z, axis=1))
    total = lax.optimization_barrier(jnp.sum(weight, axis=1))
    hess_xx = second * lax.optimization_barrier(jnp.sum(weight * off_x * off_x, axis=1)) + first * total
    hess_yy = second * lax.optimization_barrier(jnp.sum(weight * off_y * off_y, axis=1)) + first * total
    hess_zz = second * lax.optimization_barrier(jnp.sum(weight * off_z * off_z, axis=1)) + first * total
    hess_xy = second * lax.optimization_barrier(jnp.sum(weight * off_x * off_y, axis=1))
    hess_xz = second * lax.optimization_barrier(jnp.sum(weight * off_x * off_z, axis=1))
    hess_yz = second * lax.optimization_barrier(jnp.sum(weight * off_y * off_z, axis=1))
    trace = hess_xx + hess_yy + hess_zz
    quad = grad_x * grad_x * hess_xx + grad_y * grad_y * hess_yy + grad_z * grad_z * hess_zz
    quad = quad + 2.0 * (grad_x * grad_y * hess_xy + grad_x * grad_z * hess_xz + grad_y * grad_z * hess_yz)
    denom = 1.0 + grad_x * grad_x + grad_y * grad_y + grad_z * grad_z
    return -(trace - quad / denom) / jnp.sqrt(denom)

def tiles(field):
    shaped = field.reshape(N_GX, CX, N_GY, CY, CZ).transpose(0, 2, 1, 3, 4)
    return shaped.reshape(N_GX, N_GY, CELLS)

def untile(tiled):
    shaped = tiled.reshape(N_GX, N_GY, CX, CY, CZ).transpose(0, 2, 1, 3, 4)
    return shaped.reshape(N_GX * CX, N_GY * CY, CZ)

def one_tile(jitter_tile, colour_tile, cells, codes, count):
    stacked = owner_rows(jitter_tile, colour_tile, cells, codes, count)
    live = jnp.arange(cells.shape[0], dtype=jnp.int32) < count
    values = curvature(stacked)
    return jnp.where(live, values, jnp.zeros_like(values))

def one_column(packed):
    return jax.vmap(one_tile)(*packed)

def add_one(base, cells, values):
    return base.at[cells].add(SIGMA * values)

def reference(jitter, colour, surface_cells, neighbours, counts, pressure, source):
    jitter_tiles = jitter.reshape(3, N_GX, CX, N_GY, CY, CZ).transpose(1, 3, 0, 2, 4, 5)
    jitter_tiles = jitter_tiles.reshape(N_GX, N_GY, 3, CELLS)
    colour_tiles = tiles(colour)
    kappa = lax.map(one_column, (jitter_tiles, colour_tiles, surface_cells, neighbours, counts))
    rhs = untile(jax.vmap(jax.vmap(add_one))(tiles(source), surface_cells, kappa))
    current = pressure
    for sweep in range(SWEEPS):
        padded = jnp.pad(current, 1)
        beside = padded[2:, 1:-1, 1:-1] + padded[:-2, 1:-1, 1:-1]
        beside = beside + padded[1:-1, 2:, 1:-1] + padded[1:-1, :-2, 1:-1]
        beside = beside + padded[1:-1, 1:-1, 2:] + padded[1:-1, 1:-1, :-2]
        current = (beside + rhs) / 6.0
    return (current, kappa)
```

```python
import functools

import jax
import jax.numpy as jnp
from jax import lax
from jax.experimental import pallas as pl
from jax.experimental.pallas import tpu as pltpu
from jax.sharding import PartitionSpec as P

SIGMA = 1.0
SMOOTH_SQ = 4.0
SLOTS = 192
LANES = 128
ROWS = 64
STEP = 24


def pieces(value):
    high = value.astype(jnp.bfloat16)
    rest = value - high.astype(jnp.float32)
    mid = rest.astype(jnp.bfloat16)
    low = (rest - mid.astype(jnp.float32)).astype(jnp.bfloat16)
    return high, mid, low


def lane_take(table, index):
    return jnp.take_along_axis(table, index, axis=1, mode="promise_in_bounds")


def final_curvature(total, gx, gy, gz, xx, yy, zz, xy, xz, yz):
    first = -2.0 / SMOOTH_SQ
    second = 4.0 / (SMOOTH_SQ * SMOOTH_SQ)
    gx, gy, gz = first * gx, first * gy, first * gz
    xx = second * xx + first * total
    yy = second * yy + first * total
    zz = second * zz + first * total
    xy, xz, yz = second * xy, second * xz, second * yz
    trace = xx + yy + zz
    quad = gx * gx * xx + gy * gy * yy + gz * gz * zz
    quad = quad + 2.0 * (gx * gy * xy + gx * gz * xz + gy * gz * yz)
    denom = 1.0 + gx * gx + gy * gy + gz * gz
    return -(trace - quad / denom) / jnp.sqrt(denom)


def curvature_kernel(
    jitter_ref, colour_ref, cells_ref, codes_ref, counts_ref, source_ref, pressure_ref,
    kappa_ref, rhs_ref, even_ref, odd_ref,
    table, hot, window, place, row, moments,
):
    zero = jnp.zeros((ROWS, LANES), jnp.bfloat16)
    for c in range(4):
        value = colour_ref[...] if c == 3 else jitter_ref[c]
        for q, piece in enumerate(pieces(value.reshape(ROWS, LANES))):
            for p in range(2):
                rows = pl.ds(c * LANES + p * ROWS, ROWS)
                table[q, rows, p * LANES : (p + 1) * LANES] = piece
                table[q, rows, (1 - p) * LANES : (2 - p) * LANES] = zero

    row[...] = jnp.zeros_like(row)
    row[0:1, 0:SLOTS] = cells_ref[0]
    cells_row = row[0:1, :]
    as_float = cells_row.astype(jnp.float32)
    for h in range(2):
        part = jnp.broadcast_to(as_float[:, h * LANES : (h + 1) * LANES], (LANES, LANES))
        turned = part.T.astype(jnp.int32)
        keep = min(LANES, SLOTS - h * LANES)
        place[h * LANES : h * LANES + keep, :] = turned[:keep]

    lane = lax.broadcasted_iota(jnp.int32, (SLOTS, LANES), 1)
    z_of = place[...] & 127
    for step in range(8):
        target = jnp.clip(z_of + (step - 3), 0, LANES - 1)
        d, p = step // 2, step % 2
        hot[d * SLOTS : (d + 1) * SLOTS, p * LANES : (p + 1) * LANES] = jnp.where(
            lane == target, 1.0, 0.0
        ).astype(jnp.bfloat16)

    contract = (((1,), (1,)), ((), ()))
    acc = lax.dot_general(hot[...], table[0], contract, preferred_element_type=jnp.float32)
    acc = acc + lax.dot_general(hot[...], table[1], contract, preferred_element_type=jnp.float32)
    acc = acc + lax.dot_general(hot[...], table[2], contract, preferred_element_type=jnp.float32)
    window[...] = acc

    lane_step = lax.broadcasted_iota(jnp.int32, (STEP, LANES), 1)

    def group(g, carry):
        start = pl.multiple_of(g * STEP, 8)
        rows = pl.ds(start, STEP)
        cell = place[rows, :]
        code = codes_ref[0, 0, rows, :]
        x, y, z = cell >> 10, (cell >> 7) & 7, cell & 127
        a = (code * 1338) >> 16
        rest = code - a * 49
        b = (rest * 9363) >> 16
        dz = rest - b * 7
        near_x = jnp.clip(x + a - 3, 0, 7)
        near_y = jnp.clip(y + b - 3, 0, 7)
        near_z = jnp.clip(z + dz - 3, 0, LANES - 1)
        index = (dz & 1) * ROWS + near_x * 8 + near_y
        centre = ROWS + (cell >> 7)
        d = dz >> 1
        low, first, third = d < 2, d < 1, d < 3
        diff = []
        for c in range(4):
            cols = slice(c * LANES, (c + 1) * LANES)
            tabs = [window[pl.ds(pl.multiple_of(k * SLOTS + start, 8), STEP), cols] for k in range(4)]
            got = [lane_take(t, index) for t in tabs]
            value = jnp.where(
                low, jnp.where(first, got[0], got[1]), jnp.where(third, got[2], got[3])
            )
            diff.append(value - lane_take(tabs[1], centre))
        ox = (near_x - x).astype(jnp.float32) + diff[0]
        oy = (near_y - y).astype(jnp.float32) + diff[1]
        oz = (near_z - z).astype(jnp.float32) + diff[2]
        w = diff[3] * jnp.exp(-(ox * ox + oy * oy + oz * oz) / SMOOTH_SQ)
        wx, wy, wz = w * ox, w * oy, w * oz
        terms = (w, wx, wy, wz, wx * ox, wy * oy, wz * oz, wx * oy, wx * oz, wy * oz)
        out = jnp.zeros((STEP, LANES), jnp.float32)
        for q, term in enumerate(terms):
            out = jnp.where(lane_step == q, jnp.sum(term, axis=1, keepdims=True), out)
        moments[rows, :] = out
        return carry

    moments[SLOTS:, :] = jnp.zeros((2 * LANES - SLOTS, LANES), jnp.float32)
    lax.fori_loop(0, SLOTS // STEP, group, 0)

    sums = jnp.concatenate([moments[0:LANES, :].T, moments[LANES:, :].T], axis=1)
    kappa = final_curvature(*[sums[q : q + 1, :] for q in range(10)])
    slot = lax.broadcasted_iota(jnp.int32, (1, 2 * LANES), 1)
    kappa = jnp.where(slot < counts_ref[0, 0], kappa, 0.0)
    kappa_ref[0] = kappa[:, :SLOTS]

    sub = lax.broadcasted_iota(jnp.int32, (ROWS, 2 * LANES), 0)
    spread = jnp.where(sub == (cells_row >> 7), SIGMA * kappa, 0.0)
    added = jnp.zeros((ROWS, LANES), jnp.float32)
    for piece in pieces(spread):
        added = added + jnp.dot(
            piece[:, :LANES], hot[SLOTS : SLOTS + LANES, LANES:], preferred_element_type=jnp.float32
        )
        added = added + jnp.dot(
            piece[:, LANES:SLOTS], hot[SLOTS + LANES : 2 * SLOTS, LANES:], preferred_element_type=jnp.float32
        )
    rhs = source_ref[...] + added.reshape(8, 8, LANES)
    rhs_ref[...] = rhs
    even = lax.rem(lax.axis_index("gx"), 2) == 0
    pressure = pressure_ref[...]

    def send(ref, high):
        ref[0:3] = jnp.where(high, pressure[5:8], pressure[0:3])
        ref[3:5] = jnp.where(high, rhs[6:8], rhs[0:2])

    send(even_ref, even)
    send(odd_ref, jnp.logical_not(even))


def curvature_call(jitter, colour, cells, codes, counts, source, pressure):
    tile = jax.ShapeDtypeStruct((8, 8, LANES), jnp.float32)
    slab = jax.ShapeDtypeStruct((5, 8, LANES), jnp.float32)
    vmem = pl.BlockSpec(memory_space=pltpu.VMEM)
    smem = pl.BlockSpec(memory_space=pltpu.SMEM)
    return pl.pallas_call(
        curvature_kernel,
        out_shape=(jax.ShapeDtypeStruct((1, 1, SLOTS), jnp.float32), tile, slab, slab),
        in_specs=[vmem, vmem, vmem, vmem, smem, vmem, vmem],
        out_specs=(vmem, vmem, vmem, vmem),
        scratch_shapes=[
            pltpu.VMEM((3, 4 * LANES, 2 * LANES), jnp.bfloat16),
            pltpu.VMEM((4 * SLOTS, 2 * LANES), jnp.bfloat16),
            pltpu.VMEM((4 * SLOTS, 4 * LANES), jnp.float32),
            pltpu.VMEM((SLOTS, LANES), jnp.int32),
            pltpu.VMEM((8, 2 * LANES), jnp.int32),
            pltpu.VMEM((2 * LANES, LANES), jnp.float32),
        ],
        compiler_params=pltpu.CompilerParams(vmem_limit_bytes=32 * 2**20),
        name="curvature",
    )(jitter, colour, cells, codes, counts, source, pressure)


def sides(first, second, even):
    return jnp.where(even, second, first), jnp.where(even, first, second)


def middle_kernel(pressure_ref, rhs_ref, xe_ref, xo_ref, even_ref, odd_ref):
    even_x = lax.rem(lax.axis_index("gx"), 2) == 0
    even_y = lax.rem(lax.axis_index("gy"), 2) == 0
    below, above = sides(xe_ref[...], xo_ref[...], even_x)
    planes = jnp.concatenate([below[1:3], pressure_ref[...], above[0:2]], axis=0)
    rhs = jnp.concatenate([below[3:5], rhs_ref[...], above[3:5]], axis=0)
    sub = lax.broadcasted_iota(jnp.int32, (1, 8, LANES), 1)
    high = jnp.where(sub >= 5, planes, pltpu.roll(rhs, 5, 1))
    low = jnp.where(sub < 3, planes, pltpu.roll(rhs, 3, 1))
    even_ref[...] = jnp.where(even_y, high, low)
    odd_ref[...] = jnp.where(even_y, low, high)


def middle_call(pressure, rhs, xe, xo):
    vmem = pl.BlockSpec(memory_space=pltpu.VMEM)
    strip = jax.ShapeDtypeStruct((12, 8, LANES), jnp.float32)
    return pl.pallas_call(
        middle_kernel,
        out_shape=(strip, strip),
        in_specs=[vmem] * 4,
        out_specs=(vmem, vmem),
        name="edges",
    )(pressure, rhs, xe, xo)


def sweeps_kernel(n_gx, n_gy, pressure_ref, rhs_ref, xe_ref, xo_ref, ye_ref, yo_ref, out_ref):
    at_x, at_y = lax.axis_index("gx"), lax.axis_index("gy")
    below, above = sides(xe_ref[...], xo_ref[...], lax.rem(at_x, 2) == 0)
    left, right = sides(ye_ref[...], yo_ref[...], lax.rem(at_y, 2) == 0)
    own = jnp.concatenate([below[0:3], pressure_ref[...], above[0:3]], axis=0)
    rhs = jnp.concatenate([below[3:5], rhs_ref[...], above[3:5]], axis=0)
    nothing = jnp.zeros((1, 8, LANES), jnp.float32)
    wide_left = jnp.concatenate([nothing, left, nothing], axis=0)
    wide_right = jnp.concatenate([nothing, right, nothing], axis=0)
    current = jnp.concatenate([wide_left, own, wide_right], axis=1)
    rhs = jnp.concatenate([pltpu.roll(left, 3, 1), rhs, pltpu.roll(right, 5, 1)], axis=1)
    lane = lax.broadcasted_iota(jnp.int32, (1, 24, LANES), 2)
    sub = lax.broadcasted_iota(jnp.int32, (1, 24, LANES), 1)
    inside = (jnp.where(at_y > 0, 0, 8) <= sub) & (sub < jnp.where(at_y < n_gy - 1, 24, 16))
    for sweep in range(3):
        mid = current[1:-1]
        beside = current[2:] + current[:-2]
        beside = beside + pltpu.roll(mid, 23, 1) + pltpu.roll(mid, 1, 1)
        beside = beside + jnp.where(lane < LANES - 1, pltpu.roll(mid, LANES - 1, 2), 0.0)
        beside = beside + jnp.where(lane > 0, pltpu.roll(mid, 1, 2), 0.0)
        current = (beside + rhs[sweep : 12 - sweep]) / 6.0
        if sweep < 2:
            count = 12 - 2 * sweep
            plane = lax.broadcasted_iota(jnp.int32, (count, 1, 1), 0) + (sweep - 2)
            held = (plane >= jnp.where(at_x > 0, -2, 0)) & (plane < jnp.where(at_x < n_gx - 1, 10, 8))
            current = jnp.where(held & inside, current, 0.0)
    out_ref[...] = current[:, 8:16, :]


def sweeps_call(n_gx, n_gy, *values):
    vmem = pl.BlockSpec(memory_space=pltpu.VMEM)
    return pl.pallas_call(
        functools.partial(sweeps_kernel, n_gx, n_gy),
        out_shape=jax.ShapeDtypeStruct((8, 8, LANES), jnp.float32),
        in_specs=[vmem] * 6,
        out_specs=vmem,
        name="sweeps",
    )(*values)


def swap(value, axis, odd):
    size = lax.axis_size(axis)
    pairs = []
    for i in range(odd, size - 1, 2):
        pairs += [(i, i + 1), (i + 1, i)]
    return lax.ppermute(value, axis, pairs)


def per_device(jitter, colour, surface_cells, neighbours, counts, pressure, source):
    kappa, rhs, even, odd = curvature_call(
        jitter, colour, surface_cells, neighbours, counts, source, pressure
    )
    xe, xo = swap(even, "gx", 0), swap(odd, "gx", 1)
    even, odd = middle_call(pressure, rhs, xe, xo)
    ye, yo = swap(even, "gy", 0), swap(odd, "gy", 1)
    out = sweeps_call(lax.axis_size("gx"), lax.axis_size("gy"), pressure, rhs, xe, xo, ye, yo)
    return out, kappa


def solution(mesh):
    placed = (
        P(None, "gx", "gy", None),
        P("gx", "gy", None),
        P("gx", "gy", None),
        P("gx", "gy", None, None),
        P("gx", "gy"),
        P("gx", "gy", None),
        P("gx", "gy", None),
    )
    return jax.shard_map(
        per_device,
        mesh=mesh,
        in_specs=placed,
        out_specs=(P("gx", "gy", None), P("gx", "gy", None)),
        check_vma=False,
    )
```

```python
import functools

import jax
import jax.numpy as jnp
from jax import lax
from jax.experimental import pallas as pl
from jax.experimental.pallas import tpu as pltpu
from jax.sharding import PartitionSpec as P

SIGMA = 1.0
SMOOTH_SQ = 4.0
SLOTS = 192
LANES = 128
ROWS = 64
STEP = 24


def pieces(value):
    high = value.astype(jnp.bfloat16)
    rest = value - high.astype(jnp.float32)
    mid = rest.astype(jnp.bfloat16)
    low = (rest - mid.astype(jnp.float32)).astype(jnp.bfloat16)
    return high, mid, low


def lane_take(table, index):
    return jnp.take_along_axis(table, index, axis=1, mode="promise_in_bounds")


def final_curvature(total, gx, gy, gz, xx, yy, zz, xy, xz, yz):
    first = -2.0 / SMOOTH_SQ
    second = 4.0 / (SMOOTH_SQ * SMOOTH_SQ)
    gx, gy, gz = first * gx, first * gy, first * gz
    xx = second * xx + first * total
    yy = second * yy + first * total
    zz = second * zz + first * total
    xy, xz, yz = second * xy, second * xz, second * yz
    trace = xx + yy + zz
    quad = gx * gx * xx + gy * gy * yy + gz * gz * zz
    quad = quad + 2.0 * (gx * gy * xy + gx * gz * xz + gy * gz * yz)
    denom = 1.0 + gx * gx + gy * gy + gz * gz
    return -(trace - quad / denom) / jnp.sqrt(denom)


def curvature_kernel(
    jitter_hbm, colour_hbm, cells_hbm, codes_hbm, counts_ref, source_hbm, pressure_hbm,
    kappa_ref, own_ref, rhs_ref, even_ref, odd_ref,
    jitter_ref, colour_ref, cells_ref, codes_ref, source_ref, arrived,
    table, hot, window, place, row, moments,
):
    copies = [
        pltpu.make_async_copy(source, target, arrived.at[i])
        for i, (source, target) in enumerate((
            (cells_hbm, cells_ref),
            (jitter_hbm, jitter_ref),
            (colour_hbm, colour_ref),
            (codes_hbm, codes_ref),
            (source_hbm, source_ref),
            (pressure_hbm, own_ref),
        ))
    ]
    for copy in copies:
        copy.start()

    copies[0].wait()
    row[...] = jnp.zeros_like(row)
    row[0:1, 0:SLOTS] = cells_ref[0]
    cells_row = row[0:1, :]
    as_float = cells_row.astype(jnp.float32)
    for h in range(2):
        part = jnp.broadcast_to(as_float[:, h * LANES : (h + 1) * LANES], (LANES, LANES))
        turned = part.T.astype(jnp.int32)
        keep = min(LANES, SLOTS - h * LANES)
        place[h * LANES : h * LANES + keep, :] = turned[:keep]

    lane = lax.broadcasted_iota(jnp.int32, (SLOTS, LANES), 1)
    z_of = place[...] & 127
    for step in range(8):
        target = jnp.clip(z_of + (step - 3), 0, LANES - 1)
        d, p = step // 2, step % 2
        hot[d * SLOTS : (d + 1) * SLOTS, p * LANES : (p + 1) * LANES] = jnp.where(
            lane == target, 1.0, 0.0
        ).astype(jnp.bfloat16)

    copies[1].wait()
    copies[2].wait()
    zero = jnp.zeros((ROWS, LANES), jnp.bfloat16)
    for c in range(4):
        value = colour_ref[...] if c == 3 else jitter_ref[c]
        for q, piece in enumerate(pieces(value.reshape(ROWS, LANES))):
            for p in range(2):
                rows = pl.ds(c * LANES + p * ROWS, ROWS)
                table[q, rows, p * LANES : (p + 1) * LANES] = piece
                table[q, rows, (1 - p) * LANES : (2 - p) * LANES] = zero

    contract = (((1,), (1,)), ((), ()))
    acc = lax.dot_general(hot[...], table[0], contract, preferred_element_type=jnp.float32)
    acc = acc + lax.dot_general(hot[...], table[1], contract, preferred_element_type=jnp.float32)
    acc = acc + lax.dot_general(hot[...], table[2], contract, preferred_element_type=jnp.float32)
    window[...] = acc

    lane_step = lax.broadcasted_iota(jnp.int32, (STEP, LANES), 1)

    def group(g, carry):
        start = pl.multiple_of(g * STEP, 8)
        rows = pl.ds(start, STEP)
        cell = place[rows, :]
        code = codes_ref[0, 0, rows, :]
        x, y, z = cell >> 10, (cell >> 7) & 7, cell & 127
        a = (code * 1338) >> 16
        rest = code - a * 49
        b = (rest * 9363) >> 16
        dz = rest - b * 7
        near_x = jnp.clip(x + a - 3, 0, 7)
        near_y = jnp.clip(y + b - 3, 0, 7)
        near_z = jnp.clip(z + dz - 3, 0, LANES - 1)
        index = (dz & 1) * ROWS + near_x * 8 + near_y
        centre = ROWS + (cell >> 7)
        d = dz >> 1
        low, first, third = d < 2, d < 1, d < 3
        diff = []
        for c in range(4):
            cols = slice(c * LANES, (c + 1) * LANES)
            tabs = [window[pl.ds(pl.multiple_of(k * SLOTS + start, 8), STEP), cols] for k in range(4)]
            got = [lane_take(t, index) for t in tabs]
            value = jnp.where(
                low, jnp.where(first, got[0], got[1]), jnp.where(third, got[2], got[3])
            )
            diff.append(value - lane_take(tabs[1], centre))
        ox = (near_x - x).astype(jnp.float32) + diff[0]
        oy = (near_y - y).astype(jnp.float32) + diff[1]
        oz = (near_z - z).astype(jnp.float32) + diff[2]
        w = diff[3] * jnp.exp(-(ox * ox + oy * oy + oz * oz) / SMOOTH_SQ)
        wx, wy, wz = w * ox, w * oy, w * oz
        terms = (w, wx, wy, wz, wx * ox, wy * oy, wz * oz, wx * oy, wx * oz, wy * oz)
        out = jnp.zeros((STEP, LANES), jnp.float32)
        for q, term in enumerate(terms):
            out = jnp.where(lane_step == q, jnp.sum(term, axis=1, keepdims=True), out)
        moments[rows, :] = out
        return carry

    moments[SLOTS:, :] = jnp.zeros((2 * LANES - SLOTS, LANES), jnp.float32)
    copies[3].wait()
    lax.fori_loop(0, SLOTS // STEP, group, 0)

    sums = jnp.concatenate([moments[0:LANES, :].T, moments[LANES:, :].T], axis=1)
    kappa = final_curvature(*[sums[q : q + 1, :] for q in range(10)])
    slot = lax.broadcasted_iota(jnp.int32, (1, 2 * LANES), 1)
    for copy in copies[4:]:
        copy.wait()
    kappa = jnp.where(slot < counts_ref[0, 0], kappa, 0.0)
    kappa_ref[0] = kappa[:, :SLOTS]

    sub = lax.broadcasted_iota(jnp.int32, (ROWS, 2 * LANES), 0)
    spread = jnp.where(sub == (cells_row >> 7), SIGMA * kappa, 0.0)
    added = jnp.zeros((ROWS, LANES), jnp.float32)
    for piece in pieces(spread):
        added = added + jnp.dot(
            piece[:, :LANES], hot[SLOTS : SLOTS + LANES, LANES:], preferred_element_type=jnp.float32
        )
        added = added + jnp.dot(
            piece[:, LANES:SLOTS], hot[SLOTS + LANES : 2 * SLOTS, LANES:], preferred_element_type=jnp.float32
        )
    rhs = source_ref[...] + added.reshape(8, 8, LANES)
    rhs_ref[...] = rhs
    even = lax.rem(lax.axis_index("gx"), 2) == 0
    pressure = own_ref[...]

    def send(ref, high):
        ref[0:3] = jnp.where(high, pressure[5:8], pressure[0:3])
        ref[3:5] = jnp.where(high, rhs[6:8], rhs[0:2])

    send(even_ref, even)
    send(odd_ref, jnp.logical_not(even))


def curvature_call(*values):
    tile = jax.ShapeDtypeStruct((8, 8, LANES), jnp.float32)
    slab = jax.ShapeDtypeStruct((5, 8, LANES), jnp.float32)
    vmem = pl.BlockSpec(memory_space=pltpu.VMEM)
    hbm = pl.BlockSpec(memory_space=pltpu.HBM)
    smem = pl.BlockSpec(memory_space=pltpu.SMEM)
    return pl.pallas_call(
        curvature_kernel,
        out_shape=(jax.ShapeDtypeStruct((1, 1, SLOTS), jnp.float32), tile, tile, slab, slab),
        in_specs=[hbm] * 4 + [smem] + [hbm] * 2,
        out_specs=(vmem,) * 5,
        scratch_shapes=[
            pltpu.VMEM((3, 8, 8, LANES), jnp.float32),
            pltpu.VMEM((8, 8, LANES), jnp.float32),
            pltpu.VMEM((1, 1, SLOTS), jnp.int32),
            pltpu.VMEM((1, 1, SLOTS, LANES), jnp.int32),
            pltpu.VMEM((8, 8, LANES), jnp.float32),
            pltpu.SemaphoreType.DMA((6,)),
            pltpu.VMEM((3, 4 * LANES, 2 * LANES), jnp.bfloat16),
            pltpu.VMEM((4 * SLOTS, 2 * LANES), jnp.bfloat16),
            pltpu.VMEM((4 * SLOTS, 4 * LANES), jnp.float32),
            pltpu.VMEM((SLOTS, LANES), jnp.int32),
            pltpu.VMEM((8, 2 * LANES), jnp.int32),
            pltpu.VMEM((2 * LANES, LANES), jnp.float32),
        ],
        compiler_params=pltpu.CompilerParams(vmem_limit_bytes=16 * 2**20),
        name="curvature",
    )(*values)


def sides(first, second, even):
    return jnp.where(even, second, first), jnp.where(even, first, second)


def middle_kernel(pressure_ref, rhs_ref, xe_ref, xo_ref, even_ref, odd_ref):
    odd_x = lax.rem(lax.axis_index("gx"), 2)
    even_y = lax.rem(lax.axis_index("gy"), 2) == 0
    below, above = sides(xe_ref[1 - odd_x], xo_ref[...], odd_x == 0)
    planes = jnp.concatenate([below[1:3], pressure_ref[...], above[0:2]], axis=0)
    rhs = jnp.concatenate([below[3:5], rhs_ref[...], above[3:5]], axis=0)
    sub = lax.broadcasted_iota(jnp.int32, (1, 8, LANES), 1)
    high = jnp.where(sub >= 5, planes, pltpu.roll(rhs, 5, 1))
    low = jnp.where(sub < 3, planes, pltpu.roll(rhs, 3, 1))
    even_ref[...] = jnp.where(even_y, high, low)
    odd_ref[...] = jnp.where(even_y, low, high)


def middle_call(pressure, rhs, xe, xo):
    vmem = pl.BlockSpec(memory_space=pltpu.VMEM)
    strip = jax.ShapeDtypeStruct((12, 8, LANES), jnp.float32)
    return pl.pallas_call(
        middle_kernel,
        out_shape=(strip, strip),
        in_specs=[vmem] * 4,
        out_specs=(vmem, vmem),
        compiler_params=pltpu.CompilerParams(vmem_limit_bytes=8 * 2**20),
        name="edges",
    )(pressure, rhs, xe, xo)


def sweeps_kernel(
    n_gx, n_gy, kappa_ref, pressure_ref, rhs_ref, xe_ref, xo_ref, ye_ref, yo_ref,
    out_ref, curvature_ref,
):
    at_x, at_y = lax.axis_index("gx"), lax.axis_index("gy")
    odd_x, odd_y = lax.rem(at_x, 2), lax.rem(at_y, 2)
    below, above = sides(xe_ref[1 - odd_x], xo_ref[...], odd_x == 0)
    left, right = sides(ye_ref[1 - odd_y], yo_ref[...], odd_y == 0)
    curvature_ref[...] = kappa_ref[...]
    own = jnp.concatenate([below[0:3], pressure_ref[...], above[0:3]], axis=0)
    rhs = jnp.concatenate([below[3:5], rhs_ref[...], above[3:5]], axis=0)
    nothing = jnp.zeros((1, 8, LANES), jnp.float32)
    wide_left = jnp.concatenate([nothing, left, nothing], axis=0)
    wide_right = jnp.concatenate([nothing, right, nothing], axis=0)
    current = jnp.concatenate([wide_left, own, wide_right], axis=1)
    rhs = jnp.concatenate([pltpu.roll(left, 3, 1), rhs, pltpu.roll(right, 5, 1)], axis=1)
    lane = lax.broadcasted_iota(jnp.int32, (1, 24, LANES), 2)
    sub = lax.broadcasted_iota(jnp.int32, (1, 24, LANES), 1)
    inside = (jnp.where(at_y > 0, 0, 8) <= sub) & (sub < jnp.where(at_y < n_gy - 1, 24, 16))
    for sweep in range(3):
        mid = current[1:-1]
        beside = current[2:] + current[:-2]
        beside = beside + pltpu.roll(mid, 23, 1) + pltpu.roll(mid, 1, 1)
        beside = beside + jnp.where(lane < LANES - 1, pltpu.roll(mid, LANES - 1, 2), 0.0)
        beside = beside + jnp.where(lane > 0, pltpu.roll(mid, 1, 2), 0.0)
        current = (beside + rhs[sweep : 12 - sweep]) / 6.0
        if sweep < 2:
            count = 12 - 2 * sweep
            plane = lax.broadcasted_iota(jnp.int32, (count, 1, 1), 0) + (sweep - 2)
            held = (plane >= jnp.where(at_x > 0, -2, 0)) & (plane < jnp.where(at_x < n_gx - 1, 10, 8))
            current = jnp.where(held & inside, current, 0.0)
    out_ref[...] = current[:, 8:16, :]


def sweeps_call(n_gx, n_gy, *values):
    vmem = pl.BlockSpec(memory_space=pltpu.VMEM)
    return pl.pallas_call(
        functools.partial(sweeps_kernel, n_gx, n_gy),
        out_shape=(
            jax.ShapeDtypeStruct((8, 8, LANES), jnp.float32),
            jax.ShapeDtypeStruct((1, 1, SLOTS), jnp.float32),
        ),
        in_specs=[vmem] * 7,
        out_specs=(vmem, vmem),
        compiler_params=pltpu.CompilerParams(vmem_limit_bytes=8 * 2**20),
        name="sweeps",
    )(*values)


def swap_odd(value, axis):
    pairs = []
    for i in range(1, lax.axis_size(axis) - 1, 2):
        pairs += [(i, i + 1), (i + 1, i)]
    return lax.ppermute(value, axis, pairs)


def gather_even(value, axis):
    groups = [[i, i + 1] for i in range(0, lax.axis_size(axis), 2)]
    return lax.all_gather(value, axis, axis=0, axis_index_groups=groups)


def held(value):
    return pltpu.with_memory_space_constraint(value, pltpu.HBM)


def per_device(jitter, colour, surface_cells, neighbours, counts, pressure, source):
    kappa, own, rhs, even, odd = curvature_call(
        held(jitter), held(colour), held(surface_cells), held(neighbours),
        counts, held(source), held(pressure),
    )
    xo, xe = swap_odd(odd, "gx"), gather_even(even, "gx")
    even, odd = middle_call(own, rhs, xe, xo)
    yo, ye = swap_odd(odd, "gy"), gather_even(even, "gy")
    return sweeps_call(
        lax.axis_size("gx"), lax.axis_size("gy"), kappa, own, rhs, xe, xo, ye, yo
    )


def solution(mesh):
    placed = (
        P(None, "gx", "gy", None),
        P("gx", "gy", None),
        P("gx", "gy", None),
        P("gx", "gy", None, None),
        P("gx", "gy"),
        P("gx", "gy", None),
        P("gx", "gy", None),
    )
    return jax.shard_map(
        per_device,
        mesh=mesh,
        in_specs=placed,
        out_specs=(P("gx", "gy", None), P("gx", "gy", None)),
        check_vma=False,
    )
```

```python
import functools

import jax
import jax.numpy as jnp
from jax import lax
from jax.experimental import pallas as pl
from jax.experimental.pallas import tpu as pltpu
from jax.sharding import PartitionSpec as P

SIGMA = 1.0
SMOOTH_SQ = 4.0
SLOTS = 192
LANES = 128
ROWS = 64
STEP = 192


def pieces(value):
    high = value.astype(jnp.bfloat16)
    rest = value - high.astype(jnp.float32)
    mid = rest.astype(jnp.bfloat16)
    low = (rest - mid.astype(jnp.float32)).astype(jnp.bfloat16)
    return high, mid, low


def lane_take(table, index):
    return jnp.take_along_axis(table, index, axis=1, mode="promise_in_bounds")


def final_curvature(total, gx, gy, gz, xx, yy, zz, xy, xz, yz):
    first = -2.0 / SMOOTH_SQ
    second = 4.0 / (SMOOTH_SQ * SMOOTH_SQ)
    gx, gy, gz = first * gx, first * gy, first * gz
    xx = second * xx + first * total
    yy = second * yy + first * total
    zz = second * zz + first * total
    xy, xz, yz = second * xy, second * xz, second * yz
    trace = xx + yy + zz
    quad = gx * gx * xx + gy * gy * yy + gz * gz * zz
    quad = quad + 2.0 * (gx * gy * xy + gx * gz * xz + gy * gz * yz)
    denom = 1.0 + gx * gx + gy * gy + gz * gz
    return -(trace - quad / denom) / jnp.sqrt(denom)


def curvature_kernel(
    jitter_hbm, colour_hbm, cells_hbm, codes_hbm, counts_ref, source_hbm, pressure_hbm,
    kappa_ref, own_ref, rhs_ref, even_ref, odd_ref,
    jitter_ref, colour_ref, cells_ref, codes_ref, source_ref, arrived,
    table, hot, window, place, row, moments,
):
    copies = [
        pltpu.make_async_copy(source, target, arrived.at[i])
        for i, (source, target) in enumerate((
            (cells_hbm, cells_ref),
            (jitter_hbm, jitter_ref),
            (colour_hbm, colour_ref),
            (codes_hbm, codes_ref),
            (source_hbm, source_ref),
            (pressure_hbm, own_ref),
        ))
    ]
    for copy in copies:
        copy.start()

    copies[0].wait()
    row[...] = jnp.zeros_like(row)
    row[0:1, 0:SLOTS] = cells_ref[0]
    cells_row = row[0:1, :]
    as_float = cells_row.astype(jnp.float32)
    for h in range(2):
        part = jnp.broadcast_to(as_float[:, h * LANES : (h + 1) * LANES], (LANES, LANES))
        turned = part.T.astype(jnp.int32)
        keep = min(LANES, SLOTS - h * LANES)
        place[h * LANES : h * LANES + keep, :] = turned[:keep]

    lane = lax.broadcasted_iota(jnp.int32, (SLOTS, LANES), 1)
    z_of = place[...] & 127
    for step in range(7):
        target = jnp.clip(z_of + (step - 3), 0, LANES - 1)
        one = jnp.where(lane == target, 1.0, 0.0).astype(jnp.bfloat16)
        for q in range(3):
            hot[step % 2, (step // 2) * SLOTS : (step // 2 + 1) * SLOTS, q * LANES : (q + 1) * LANES] = one

    copies[1].wait()
    copies[2].wait()
    for c in range(4):
        value = colour_ref[...] if c == 3 else jitter_ref[c]
        for q, piece in enumerate(pieces(value.reshape(ROWS, LANES))):
            columns = slice(q * LANES, (q + 1) * LANES)
            table[0, c * ROWS : (c + 1) * ROWS, columns] = piece
            table[1, (c ^ 1) * ROWS : ((c ^ 1) + 1) * ROWS, columns] = piece

    contract = (((1,), (1,)), ((), ()))
    window[0] = lax.dot_general(hot[0], table[0], contract, preferred_element_type=jnp.float32)
    window[1, : 3 * SLOTS] = lax.dot_general(
        hot[1, : 3 * SLOTS], table[1], contract, preferred_element_type=jnp.float32
    )

    lane_step = lax.broadcasted_iota(jnp.int32, (STEP, LANES), 1)

    def group(g, carry):
        start = pl.multiple_of(g * STEP, 8)
        rows = pl.ds(start, STEP)
        cell = place[rows, :]
        code = codes_ref[0, 0, rows, :]
        x, y, z = cell >> 10, (cell >> 7) & 7, cell & 127
        a = (code * 1338) >> 16
        rest = code - a * 49
        b = (rest * 9363) >> 16
        dz = rest - b * 7
        near_x = jnp.clip(x + a - 3, 0, 7)
        near_y = jnp.clip(y + b - 3, 0, 7)
        near_z = jnp.clip(z + dz - 3, 0, LANES - 1)
        near = near_x * 8 + near_y
        index = (near + (dz & 1) * ROWS, near + (1 - (dz & 1)) * ROWS)
        own = cell >> 7
        centre = (own + ROWS, own)
        d = dz >> 1
        low, first, third = d < 2, d < 1, d < 3
        left = lane_step < ROWS
        tabs = []
        for k in range(4):
            at = pl.ds(pl.multiple_of(k * SLOTS + start, 8), STEP)
            for pair in range(2):
                cols = slice(pair * LANES, (pair + 1) * LANES)
                even = window[0, at, cols]
                odd = window[1, at, cols] if k < 3 else even
                tabs.append((jnp.where(left, even, odd), jnp.where(left, odd, even)))
        diff = []
        for c in range(4):
            mine = [tabs[2 * k + c // 2][c % 2] for k in range(4)]
            got = [lane_take(t, index[c % 2]) for t in mine]
            value = jnp.where(
                low, jnp.where(first, got[0], got[1]), jnp.where(third, got[2], got[3])
            )
            diff.append(value - lane_take(mine[1], centre[c % 2]))
        ox = (near_x - x).astype(jnp.float32) + diff[0]
        oy = (near_y - y).astype(jnp.float32) + diff[1]
        oz = (near_z - z).astype(jnp.float32) + diff[2]
        w = diff[3] * jnp.exp(-(ox * ox + oy * oy + oz * oz) / SMOOTH_SQ)
        wx, wy, wz = w * ox, w * oy, w * oz
        terms = (w, wx, wy, wz, wx * ox, wy * oy, wz * oz, wx * oy, wx * oz, wy * oz)
        out = jnp.zeros((STEP, LANES), jnp.float32)
        for q, term in enumerate(terms):
            out = jnp.where(lane_step == q, jnp.sum(term, axis=1, keepdims=True), out)
        moments[rows, :] = out
        return carry

    moments[SLOTS:, :] = jnp.zeros((2 * LANES - SLOTS, LANES), jnp.float32)
    copies[3].wait()
    lax.fori_loop(0, SLOTS // STEP, group, 0)

    sums = jnp.concatenate([moments[0:LANES, :].T, moments[LANES:, :].T], axis=1)
    kappa = final_curvature(*[sums[q : q + 1, :] for q in range(10)])
    slot = lax.broadcasted_iota(jnp.int32, (1, 2 * LANES), 1)
    for copy in copies[4:]:
        copy.wait()
    kappa = jnp.where(slot < counts_ref[0, 0], kappa, 0.0)
    kappa_ref[0] = kappa[:, :SLOTS]

    sub = lax.broadcasted_iota(jnp.int32, (ROWS, 2 * LANES), 0)
    spread = jnp.where(sub == (cells_row >> 7), SIGMA * kappa, 0.0)
    added = jnp.zeros((ROWS, LANES), jnp.float32)
    for piece in pieces(spread):
        added = added + jnp.dot(
            piece[:, :LANES], hot[1, SLOTS : SLOTS + LANES, :LANES], preferred_element_type=jnp.float32
        )
        added = added + jnp.dot(
            piece[:, LANES:SLOTS], hot[1, SLOTS + LANES : 2 * SLOTS, :LANES], preferred_element_type=jnp.float32
        )
    rhs = source_ref[...] + added.reshape(8, 8, LANES)
    rhs_ref[...] = rhs
    even = lax.rem(lax.axis_index("gx"), 2) == 0
    pressure = own_ref[...]

    def send(ref, high):
        ref[0:3] = jnp.where(high, pressure[5:8], pressure[0:3])
        ref[3:5] = jnp.where(high, rhs[6:8], rhs[0:2])

    send(even_ref, even)
    send(odd_ref, jnp.logical_not(even))


def curvature_call(*values):
    tile = jax.ShapeDtypeStruct((8, 8, LANES), jnp.float32)
    slab = jax.ShapeDtypeStruct((5, 8, LANES), jnp.float32)
    vmem = pl.BlockSpec(memory_space=pltpu.VMEM)
    hbm = pl.BlockSpec(memory_space=pltpu.HBM)
    smem = pl.BlockSpec(memory_space=pltpu.SMEM)
    return pl.pallas_call(
        curvature_kernel,
        out_shape=(jax.ShapeDtypeStruct((1, 1, SLOTS), jnp.float32), tile, tile, slab, slab),
        in_specs=[hbm] * 4 + [smem] + [hbm] * 2,
        out_specs=(vmem,) * 5,
        scratch_shapes=[
            pltpu.VMEM((3, 8, 8, LANES), jnp.float32),
            pltpu.VMEM((8, 8, LANES), jnp.float32),
            pltpu.VMEM((1, 1, SLOTS), jnp.int32),
            pltpu.VMEM((1, 1, SLOTS, LANES), jnp.int32),
            pltpu.VMEM((8, 8, LANES), jnp.float32),
            pltpu.SemaphoreType.DMA((6,)),
            pltpu.VMEM((2, 4 * ROWS, 3 * LANES), jnp.bfloat16),
            pltpu.VMEM((2, 4 * SLOTS, 3 * LANES), jnp.bfloat16),
            pltpu.VMEM((2, 4 * SLOTS, 4 * ROWS), jnp.float32),
            pltpu.VMEM((SLOTS, LANES), jnp.int32),
            pltpu.VMEM((8, 2 * LANES), jnp.int32),
            pltpu.VMEM((2 * LANES, LANES), jnp.float32),
        ],
        compiler_params=pltpu.CompilerParams(vmem_limit_bytes=16 * 2**20),
        name="curvature",
    )(*values)


def sides(first, second, even):
    return jnp.where(even, second, first), jnp.where(even, first, second)


def middle_kernel(pressure_ref, rhs_ref, xe_ref, xo_ref, even_ref, odd_ref):
    odd_x = lax.rem(lax.axis_index("gx"), 2)
    even_y = lax.rem(lax.axis_index("gy"), 2) == 0
    below, above = sides(xe_ref[1 - odd_x], xo_ref[...], odd_x == 0)
    planes = jnp.concatenate([below[1:3], pressure_ref[...], above[0:2]], axis=0)
    rhs = jnp.concatenate([below[3:5], rhs_ref[...], above[3:5]], axis=0)
    sub = lax.broadcasted_iota(jnp.int32, (1, 8, LANES), 1)
    high = jnp.where(sub >= 5, planes, pltpu.roll(rhs, 5, 1))
    low = jnp.where(sub < 3, planes, pltpu.roll(rhs, 3, 1))
    even_ref[...] = jnp.where(even_y, high, low)
    odd_ref[...] = jnp.where(even_y, low, high)


def middle_call(pressure, rhs, xe, xo):
    vmem = pl.BlockSpec(memory_space=pltpu.VMEM)
    strip = jax.ShapeDtypeStruct((12, 8, LANES), jnp.float32)
    return pl.pallas_call(
        middle_kernel,
        out_shape=(strip, strip),
        in_specs=[vmem] * 4,
        out_specs=(vmem, vmem),
        compiler_params=pltpu.CompilerParams(vmem_limit_bytes=8 * 2**20),
        name="edges",
    )(pressure, rhs, xe, xo)


def sweeps_kernel(
    n_gx, n_gy, kappa_ref, pressure_ref, rhs_ref, xe_ref, xo_ref, ye_ref, yo_ref,
    out_ref, curvature_ref,
):
    at_x, at_y = lax.axis_index("gx"), lax.axis_index("gy")
    odd_x, odd_y = lax.rem(at_x, 2), lax.rem(at_y, 2)
    below, above = sides(xe_ref[1 - odd_x], xo_ref[...], odd_x == 0)
    left, right = sides(ye_ref[1 - odd_y], yo_ref[...], odd_y == 0)
    curvature_ref[...] = kappa_ref[...]
    own = jnp.concatenate([below[0:3], pressure_ref[...], above[0:3]], axis=0)
    rhs = jnp.concatenate([below[3:5], rhs_ref[...], above[3:5]], axis=0)
    nothing = jnp.zeros((1, 8, LANES), jnp.float32)
    wide_left = jnp.concatenate([nothing, left, nothing], axis=0)
    wide_right = jnp.concatenate([nothing, right, nothing], axis=0)
    current = jnp.concatenate([wide_left, own, wide_right], axis=1)
    rhs = jnp.concatenate([pltpu.roll(left, 3, 1), rhs, pltpu.roll(right, 5, 1)], axis=1)
    lane = lax.broadcasted_iota(jnp.int32, (1, 24, LANES), 2)
    sub = lax.broadcasted_iota(jnp.int32, (1, 24, LANES), 1)
    inside = (jnp.where(at_y > 0, 0, 8) <= sub) & (sub < jnp.where(at_y < n_gy - 1, 24, 16))
    for sweep in range(3):
        mid = current[1:-1]
        beside = current[2:] + current[:-2]
        beside = beside + pltpu.roll(mid, 23, 1) + pltpu.roll(mid, 1, 1)
        beside = beside + jnp.where(lane < LANES - 1, pltpu.roll(mid, LANES - 1, 2), 0.0)
        beside = beside + jnp.where(lane > 0, pltpu.roll(mid, 1, 2), 0.0)
        current = (beside + rhs[sweep : 12 - sweep]) / 6.0
        if sweep < 2:
            count = 12 - 2 * sweep
            plane = lax.broadcasted_iota(jnp.int32, (count, 1, 1), 0) + (sweep - 2)
            held = (plane >= jnp.where(at_x > 0, -2, 0)) & (plane < jnp.where(at_x < n_gx - 1, 10, 8))
            current = jnp.where(held & inside, current, 0.0)
    out_ref[...] = current[:, 8:16, :]


def sweeps_call(n_gx, n_gy, *values):
    vmem = pl.BlockSpec(memory_space=pltpu.VMEM)
    return pl.pallas_call(
        functools.partial(sweeps_kernel, n_gx, n_gy),
        out_shape=(
            jax.ShapeDtypeStruct((8, 8, LANES), jnp.float32),
            jax.ShapeDtypeStruct((1, 1, SLOTS), jnp.float32),
        ),
        in_specs=[vmem] * 7,
        out_specs=(vmem, vmem),
        compiler_params=pltpu.CompilerParams(vmem_limit_bytes=8 * 2**20),
        name="sweeps",
    )(*values)


def swap_odd(value, axis):
    pairs = []
    for i in range(1, lax.axis_size(axis) - 1, 2):
        pairs += [(i, i + 1), (i + 1, i)]
    return lax.ppermute(value, axis, pairs)


def gather_even(value, axis):
    groups = [[i, i + 1] for i in range(0, lax.axis_size(axis), 2)]
    return lax.all_gather(value, axis, axis=0, axis_index_groups=groups)


def held(value):
    return pltpu.with_memory_space_constraint(value, pltpu.HBM)


def per_device(jitter, colour, surface_cells, neighbours, counts, pressure, source):
    kappa, own, rhs, even, odd = curvature_call(
        held(jitter), held(colour), held(surface_cells), held(neighbours),
        counts, held(source), held(pressure),
    )
    xo, xe = swap_odd(odd, "gx"), gather_even(even, "gx")
    even, odd = middle_call(own, rhs, xe, xo)
    yo, ye = swap_odd(odd, "gy"), gather_even(even, "gy")
    return sweeps_call(
        lax.axis_size("gx"), lax.axis_size("gy"), kappa, own, rhs, xe, xo, ye, yo
    )


def solution(mesh):
    placed = (
        P(None, "gx", "gy", None),
        P("gx", "gy", None),
        P("gx", "gy", None),
        P("gx", "gy", None, None),
        P("gx", "gy"),
        P("gx", "gy", None),
        P("gx", "gy", None),
    )
    return jax.shard_map(
        per_device,
        mesh=mesh,
        in_specs=placed,
        out_specs=(P("gx", "gy", None), P("gx", "gy", None)),
        check_vma=False,
    )
```

```python
import functools

import jax
import jax.numpy as jnp
from jax import lax
from jax.experimental import pallas as pl
from jax.experimental.pallas import tpu as pltpu
from jax.sharding import PartitionSpec as P

SIGMA = 1.0
SMOOTH_SQ = 4.0
SLOTS = 192
LANES = 128
ROWS = 64
STEP = 192
SCALE = 32767.0 / 0.3


def pieces(value):
    high = value.astype(jnp.bfloat16)
    rest = value - high.astype(jnp.float32)
    mid = rest.astype(jnp.bfloat16)
    low = (rest - mid.astype(jnp.float32)).astype(jnp.bfloat16)
    return high, mid, low


def lane_take(table, index):
    return jnp.take_along_axis(table, index, axis=1, mode="promise_in_bounds")


def final_curvature(total, gx, gy, gz, xx, yy, zz, xy, xz, yz):
    first = -2.0 / SMOOTH_SQ
    second = 4.0 / (SMOOTH_SQ * SMOOTH_SQ)
    gx, gy, gz = first * gx, first * gy, first * gz
    xx = second * xx + first * total
    yy = second * yy + first * total
    zz = second * zz + first * total
    xy, xz, yz = second * xy, second * xz, second * yz
    trace = xx + yy + zz
    quad = gx * gx * xx + gy * gy * yy + gz * gz * zz
    quad = quad + 2.0 * (gx * gy * xy + gx * gz * xz + gy * gz * yz)
    denom = 1.0 + gx * gx + gy * gy + gz * gz
    return -(trace - quad / denom) / jnp.sqrt(denom)


def curvature_kernel(
    jitter_hbm, colour_hbm, cells_hbm, codes_hbm, counts_ref, source_hbm, pressure_hbm,
    kappa_ref, own_ref, rhs_ref, even_ref, odd_ref,
    jitter_ref, colour_ref, cells_ref, codes_ref, source_ref, arrived,
    table, hot, window, place, row, moments,
):
    copies = [
        pltpu.make_async_copy(source, target, arrived.at[i])
        for i, (source, target) in enumerate((
            (cells_hbm, cells_ref),
            (jitter_hbm, jitter_ref),
            (colour_hbm, colour_ref),
            (codes_hbm, codes_ref),
            (source_hbm, source_ref),
            (pressure_hbm, own_ref),
        ))
    ]
    for copy in copies:
        copy.start()

    copies[0].wait()
    row[...] = jnp.zeros_like(row)
    row[0:1, 0:SLOTS] = cells_ref[0]
    cells_row = row[0:1, :]
    as_float = cells_row.astype(jnp.float32)
    for h in range(2):
        part = jnp.broadcast_to(as_float[:, h * LANES : (h + 1) * LANES], (LANES, LANES))
        turned = part.T.astype(jnp.int32)
        keep = min(LANES, SLOTS - h * LANES)
        place[h * LANES : h * LANES + keep, :] = turned[:keep]

    lane = lax.broadcasted_iota(jnp.int32, (SLOTS, LANES), 1)
    z_of = place[...] & 127
    for step in range(7):
        target = jnp.clip(z_of + (step - 3), 0, LANES - 1)
        one = jnp.where(lane == target, 1.0, 0.0).astype(jnp.bfloat16)
        for q in range(3):
            hot[step % 2, (step // 2) * SLOTS : (step // 2 + 1) * SLOTS, q * LANES : (q + 1) * LANES] = one

    for copy in copies[1:]:
        copy.wait()
    whole_x = jnp.round(jitter_ref[0] * SCALE)
    whole_y = jnp.round(jitter_ref[1] * SCALE) + 32768.0
    for c, value in enumerate((whole_x, jitter_ref[2], whole_y, colour_ref[...])):
        for q, piece in enumerate(pieces(value.reshape(ROWS, LANES))):
            columns = slice(q * LANES, (q + 1) * LANES)
            table[0, c * ROWS : (c + 1) * ROWS, columns] = piece
            table[1, (c ^ 1) * ROWS : ((c ^ 1) + 1) * ROWS, columns] = piece

    contract = (((1,), (1,)), ((), ()))
    window[0] = lax.dot_general(hot[0], table[0], contract, preferred_element_type=jnp.float32)
    window[1, : 3 * SLOTS] = lax.dot_general(
        hot[1, : 3 * SLOTS], table[1], contract, preferred_element_type=jnp.float32
    )

    lane_step = lax.broadcasted_iota(jnp.int32, (STEP, LANES), 1)

    def group(g, carry):
        start = 0
        rows = pl.ds(start, STEP)
        cell = place[rows, :]
        code = codes_ref[0, 0, rows, :]
        x, y, z = cell >> 10, (cell >> 7) & 7, cell & 127
        a = (code * 1338) >> 16
        rest = code - a * 49
        b = (rest * 9363) >> 16
        dz = rest - b * 7
        near_x = jnp.clip(x + a - 3, 0, 7)
        near_y = jnp.clip(y + b - 3, 0, 7)
        near_z = jnp.clip(z + dz - 3, 0, LANES - 1)
        near = near_x * 8 + near_y
        index = (near + (dz & 1) * ROWS, near + (1 - (dz & 1)) * ROWS)
        own = cell >> 7
        centre = (own + ROWS, own)
        d = dz >> 1
        low, first, third = d < 2, d < 1, d < 3
        left = lane_step < ROWS
        both, third_of, colour_of = [], [], []
        for k in range(4):
            at = pl.ds(k * SLOTS, STEP)
            even = [window[0, at, p * LANES : (p + 1) * LANES] for p in range(2)]
            odd = [window[1, at, p * LANES : (p + 1) * LANES] for p in range(2)] if k < 3 else even
            x_whole = jnp.where(left, even[0], odd[0]).astype(jnp.int32)
            y_whole = jnp.where(left, even[1], odd[1]).astype(jnp.int32)
            both.append((x_whole << 16) | y_whole)
            third_of.append(jnp.where(left, odd[0], even[0]))
            colour_of.append(jnp.where(left, odd[1], even[1]))

        def pick(tabs, swapped):
            got = [lane_take(t, index[swapped]) for t in tabs]
            value = jnp.where(
                low, jnp.where(first, got[0], got[1]), jnp.where(third, got[2], got[3])
            )
            return value, lane_take(tabs[1], centre[swapped])

        at_near, at_own = pick(both, 0)
        z_near, z_own = pick(third_of, 1)
        c_near, c_own = pick(colour_of, 1)
        diff = (
            ((at_near >> 16) - (at_own >> 16)).astype(jnp.float32) * (1.0 / SCALE),
            ((at_near & 65535) - (at_own & 65535)).astype(jnp.float32) * (1.0 / SCALE),
            z_near - z_own,
            c_near - c_own,
        )
        ox = (near_x - x).astype(jnp.float32) + diff[0]
        oy = (near_y - y).astype(jnp.float32) + diff[1]
        oz = (near_z - z).astype(jnp.float32) + diff[2]
        w = diff[3] * jnp.exp(-(ox * ox + oy * oy + oz * oz) / SMOOTH_SQ)
        wx, wy, wz = w * ox, w * oy, w * oz
        terms = (w, wx, wy, wz, wx * ox, wy * oy, wz * oz, wx * oy, wx * oz, wy * oz)
        out = jnp.zeros((STEP, LANES), jnp.float32)
        for q, term in enumerate(terms):
            out = jnp.where(lane_step == q, jnp.sum(term, axis=1, keepdims=True), out)
        moments[rows, :] = out
        return carry

    moments[SLOTS:, :] = jnp.zeros((2 * LANES - SLOTS, LANES), jnp.float32)
    group(0, 0)

    sums = jnp.concatenate([moments[0:LANES, :].T, moments[LANES:, :].T], axis=1)
    kappa = final_curvature(*[sums[q : q + 1, :] for q in range(10)])
    slot = lax.broadcasted_iota(jnp.int32, (1, 2 * LANES), 1)
    kappa = jnp.where(slot < counts_ref[0, 0], kappa, 0.0)
    kappa_ref[0] = kappa[:, :SLOTS]

    sub = lax.broadcasted_iota(jnp.int32, (ROWS, 2 * LANES), 0)
    spread = jnp.where(sub == (cells_row >> 7), SIGMA * kappa, 0.0)
    added = jnp.zeros((ROWS, LANES), jnp.float32)
    for piece in pieces(spread):
        added = added + jnp.dot(
            piece[:, :LANES], hot[1, SLOTS : SLOTS + LANES, :LANES], preferred_element_type=jnp.float32
        )
        added = added + jnp.dot(
            piece[:, LANES:SLOTS], hot[1, SLOTS + LANES : 2 * SLOTS, :LANES], preferred_element_type=jnp.float32
        )
    rhs = source_ref[...] + added.reshape(8, 8, LANES)
    rhs_ref[...] = rhs
    even = lax.rem(lax.axis_index("gx"), 2) == 0
    pressure = own_ref[...]

    def send(ref, high):
        ref[0:3] = jnp.where(high, pressure[5:8], pressure[0:3])
        ref[3:5] = jnp.where(high, rhs[6:8], rhs[0:2])

    send(even_ref, even)
    send(odd_ref, jnp.logical_not(even))


def curvature_call(*values):
    tile = jax.ShapeDtypeStruct((8, 8, LANES), jnp.float32)
    slab = jax.ShapeDtypeStruct((5, 8, LANES), jnp.float32)
    vmem = pl.BlockSpec(memory_space=pltpu.VMEM)
    hbm = pl.BlockSpec(memory_space=pltpu.HBM)
    smem = pl.BlockSpec(memory_space=pltpu.SMEM)
    return pl.pallas_call(
        curvature_kernel,
        out_shape=(jax.ShapeDtypeStruct((1, 1, SLOTS), jnp.float32), tile, tile, slab, slab),
        in_specs=[hbm] * 4 + [smem] + [hbm] * 2,
        out_specs=(vmem,) * 5,
        scratch_shapes=[
            pltpu.VMEM((3, 8, 8, LANES), jnp.float32),
            pltpu.VMEM((8, 8, LANES), jnp.float32),
            pltpu.VMEM((1, 1, SLOTS), jnp.int32),
            pltpu.VMEM((1, 1, SLOTS, LANES), jnp.int32),
            pltpu.VMEM((8, 8, LANES), jnp.float32),
            pltpu.SemaphoreType.DMA((6,)),
            pltpu.VMEM((2, 4 * ROWS, 3 * LANES), jnp.bfloat16),
            pltpu.VMEM((2, 4 * SLOTS, 3 * LANES), jnp.bfloat16),
            pltpu.VMEM((2, 4 * SLOTS, 4 * ROWS), jnp.float32),
            pltpu.VMEM((SLOTS, LANES), jnp.int32),
            pltpu.VMEM((8, 2 * LANES), jnp.int32),
            pltpu.VMEM((2 * LANES, LANES), jnp.float32),
        ],
        compiler_params=pltpu.CompilerParams(vmem_limit_bytes=16 * 2**20),
        name="curvature",
    )(*values)


def sides(first, second, even):
    return jnp.where(even, second, first), jnp.where(even, first, second)


def middle_kernel(pressure_ref, rhs_ref, xe_ref, xo_ref, even_ref, odd_ref):
    odd_x = lax.rem(lax.axis_index("gx"), 2)
    even_y = lax.rem(lax.axis_index("gy"), 2) == 0
    below, above = sides(xe_ref[1 - odd_x], xo_ref[...], odd_x == 0)
    planes = jnp.concatenate([below[1:3], pressure_ref[...], above[0:2]], axis=0)
    rhs = jnp.concatenate([below[3:5], rhs_ref[...], above[3:5]], axis=0)
    sub = lax.broadcasted_iota(jnp.int32, (1, 8, LANES), 1)
    high = jnp.where(sub >= 5, planes, pltpu.roll(rhs, 5, 1))
    low = jnp.where(sub < 3, planes, pltpu.roll(rhs, 3, 1))
    even_ref[...] = jnp.where(even_y, high, low)
    odd_ref[...] = jnp.where(even_y, low, high)


def middle_call(pressure, rhs, xe, xo):
    vmem = pl.BlockSpec(memory_space=pltpu.VMEM)
    strip = jax.ShapeDtypeStruct((12, 8, LANES), jnp.float32)
    return pl.pallas_call(
        middle_kernel,
        out_shape=(strip, strip),
        in_specs=[vmem] * 4,
        out_specs=(vmem, vmem),
        compiler_params=pltpu.CompilerParams(vmem_limit_bytes=8 * 2**20),
        name="edges",
    )(pressure, rhs, xe, xo)


def sweeps_kernel(
    n_gx, n_gy, kappa_ref, pressure_ref, rhs_ref, xe_ref, xo_ref, ye_ref, yo_ref,
    out_ref, curvature_ref,
):
    at_x, at_y = lax.axis_index("gx"), lax.axis_index("gy")
    odd_x, odd_y = lax.rem(at_x, 2), lax.rem(at_y, 2)
    below, above = sides(xe_ref[1 - odd_x], xo_ref[...], odd_x == 0)
    left, right = sides(ye_ref[1 - odd_y], yo_ref[...], odd_y == 0)
    curvature_ref[...] = kappa_ref[...]
    own = jnp.concatenate([below[0:3], pressure_ref[...], above[0:3]], axis=0)
    rhs = jnp.concatenate([below[3:5], rhs_ref[...], above[3:5]], axis=0)
    nothing = jnp.zeros((1, 8, LANES), jnp.float32)
    wide_left = jnp.concatenate([nothing, left, nothing], axis=0)
    wide_right = jnp.concatenate([nothing, right, nothing], axis=0)
    current = jnp.concatenate([wide_left, own, wide_right], axis=1)
    rhs = jnp.concatenate([pltpu.roll(left, 3, 1), rhs, pltpu.roll(right, 5, 1)], axis=1)
    lane = lax.broadcasted_iota(jnp.int32, (1, 24, LANES), 2)
    sub = lax.broadcasted_iota(jnp.int32, (1, 24, LANES), 1)
    inside = (jnp.where(at_y > 0, 0, 8) <= sub) & (sub < jnp.where(at_y < n_gy - 1, 24, 16))
    for sweep in range(3):
        mid = current[1:-1]
        beside = current[2:] + current[:-2]
        beside = beside + pltpu.roll(mid, 23, 1) + pltpu.roll(mid, 1, 1)
        beside = beside + jnp.where(lane < LANES - 1, pltpu.roll(mid, LANES - 1, 2), 0.0)
        beside = beside + jnp.where(lane > 0, pltpu.roll(mid, 1, 2), 0.0)
        current = (beside + rhs[sweep : 12 - sweep]) / 6.0
        if sweep < 2:
            count = 12 - 2 * sweep
            plane = lax.broadcasted_iota(jnp.int32, (count, 1, 1), 0) + (sweep - 2)
            held = (plane >= jnp.where(at_x > 0, -2, 0)) & (plane < jnp.where(at_x < n_gx - 1, 10, 8))
            current = jnp.where(held & inside, current, 0.0)
    out_ref[...] = current[:, 8:16, :]


def sweeps_call(n_gx, n_gy, *values):
    vmem = pl.BlockSpec(memory_space=pltpu.VMEM)
    return pl.pallas_call(
        functools.partial(sweeps_kernel, n_gx, n_gy),
        out_shape=(
            jax.ShapeDtypeStruct((8, 8, LANES), jnp.float32),
            jax.ShapeDtypeStruct((1, 1, SLOTS), jnp.float32),
        ),
        in_specs=[vmem] * 7,
        out_specs=(vmem, vmem),
        compiler_params=pltpu.CompilerParams(vmem_limit_bytes=8 * 2**20),
        name="sweeps",
    )(*values)


def swap_odd(value, axis):
    pairs = []
    for i in range(1, lax.axis_size(axis) - 1, 2):
        pairs += [(i, i + 1), (i + 1, i)]
    return lax.ppermute(value, axis, pairs)


def gather_even(value, axis):
    groups = [[i, i + 1] for i in range(0, lax.axis_size(axis), 2)]
    return lax.all_gather(value, axis, axis=0, axis_index_groups=groups)


def held(value):
    return pltpu.with_memory_space_constraint(value, pltpu.HBM)


def per_device(jitter, colour, surface_cells, neighbours, counts, pressure, source):
    kappa, own, rhs, even, odd = curvature_call(
        held(jitter), held(colour), held(surface_cells), held(neighbours),
        counts, held(source), held(pressure),
    )
    xo, xe = swap_odd(odd, "gx"), gather_even(even, "gx")
    even, odd = middle_call(own, rhs, xe, xo)
    yo, ye = swap_odd(odd, "gy"), gather_even(even, "gy")
    return sweeps_call(
        lax.axis_size("gx"), lax.axis_size("gy"), kappa, own, rhs, xe, xo, ye, yo
    )


def solution(mesh):
    placed = (
        P(None, "gx", "gy", None),
        P("gx", "gy", None),
        P("gx", "gy", None),
        P("gx", "gy", None, None),
        P("gx", "gy"),
        P("gx", "gy", None),
        P("gx", "gy", None),
    )
    return jax.shard_map(
        per_device,
        mesh=mesh,
        in_specs=placed,
        out_specs=(P("gx", "gy", None), P("gx", "gy", None)),
        check_vma=False,
    )
```

```python
import functools

import jax
import jax.numpy as jnp
from jax import lax
from jax.experimental import pallas as pl
from jax.experimental.pallas import tpu as pltpu
from jax.sharding import PartitionSpec as P

SIGMA = 1.0
SMOOTH_SQ = 4.0
SLOTS = 192
LANES = 128
ROWS = 64
STEP = 192
SCALE = 32767.0 / 0.3


def pieces(value):
    high = value.astype(jnp.bfloat16)
    rest = value - high.astype(jnp.float32)
    mid = rest.astype(jnp.bfloat16)
    low = (rest - mid.astype(jnp.float32)).astype(jnp.bfloat16)
    return high, mid, low


def lane_take(table, index):
    return jnp.take_along_axis(table, index, axis=1, mode="promise_in_bounds")


def final_curvature(total, gx, gy, gz, xx, yy, zz, xy, xz, yz):
    first = -2.0 / SMOOTH_SQ
    second = 4.0 / (SMOOTH_SQ * SMOOTH_SQ)
    gx, gy, gz = first * gx, first * gy, first * gz
    xx = second * xx + first * total
    yy = second * yy + first * total
    zz = second * zz + first * total
    xy, xz, yz = second * xy, second * xz, second * yz
    trace = xx + yy + zz
    quad = gx * gx * xx + gy * gy * yy + gz * gz * zz
    quad = quad + 2.0 * (gx * gy * xy + gx * gz * xz + gy * gz * yz)
    denom = 1.0 + gx * gx + gy * gy + gz * gz
    return -(trace - quad / denom) / jnp.sqrt(denom)


def curvature_kernel(
    jitter_hbm, colour_hbm, cells_hbm, codes_hbm, counts_ref, source_hbm, pressure_hbm,
    kappa_ref, own_ref, rhs_ref, even_ref, odd_ref,
    jitter_ref, colour_ref, cells_ref, codes_ref, source_ref, arrived,
    table, hot, window, place, row, moments,
):
    copies = [
        pltpu.make_async_copy(source, target, arrived.at[i])
        for i, (source, target) in enumerate((
            (cells_hbm, cells_ref),
            (jitter_hbm, jitter_ref),
            (colour_hbm, colour_ref),
            (codes_hbm, codes_ref),
            (source_hbm, source_ref),
            (pressure_hbm, own_ref),
        ))
    ]
    for copy in copies:
        copy.start()

    copies[0].wait()
    row[...] = jnp.zeros_like(row)
    row[0:1, 0:SLOTS] = cells_ref[0]
    cells_row = row[0:1, :]
    as_float = cells_row.astype(jnp.float32)
    for h in range(2):
        part = jnp.broadcast_to(as_float[:, h * LANES : (h + 1) * LANES], (LANES, LANES))
        turned = part.T.astype(jnp.int32)
        keep = min(LANES, SLOTS - h * LANES)
        place[h * LANES : h * LANES + keep, :] = turned[:keep]

    lane = lax.broadcasted_iota(jnp.int32, (SLOTS, LANES), 1)
    z_of = place[...] & 127
    for step in range(7):
        target = jnp.clip(z_of + (step - 3), 0, LANES - 1)
        one = jnp.where(lane == target, 1.0, 0.0).astype(jnp.bfloat16)
        for q in range(3):
            hot[step % 2, (step // 2) * SLOTS : (step // 2 + 1) * SLOTS, q * LANES : (q + 1) * LANES] = one

    for copy in copies[1:]:
        copy.wait()
    whole_x = jnp.round(jitter_ref[0] * SCALE)
    whole_y = jnp.round(jitter_ref[1] * SCALE) + 32768.0
    for c, value in enumerate((whole_x, jitter_ref[2], whole_y, colour_ref[...])):
        for q, piece in enumerate(pieces(value.reshape(ROWS, LANES))):
            columns = slice(q * LANES, (q + 1) * LANES)
            table[0, c * ROWS : (c + 1) * ROWS, columns] = piece
            table[1, (c ^ 1) * ROWS : ((c ^ 1) + 1) * ROWS, columns] = piece

    contract = (((1,), (1,)), ((), ()))
    window[0] = lax.dot_general(hot[0], table[0], contract, preferred_element_type=jnp.float32)
    window[1, : 3 * SLOTS] = lax.dot_general(
        hot[1, : 3 * SLOTS], table[1], contract, preferred_element_type=jnp.float32
    )

    lane_step = lax.broadcasted_iota(jnp.int32, (STEP, LANES), 1)

    def group(g, carry):
        start = 0
        rows = pl.ds(start, STEP)
        cell = place[rows, :]
        code = codes_ref[0, 0, rows, :]
        x, y, z = cell >> 10, (cell >> 7) & 7, cell & 127
        a = (code * 1338) >> 16
        rest = code - a * 49
        b = (rest * 9363) >> 16
        dz = rest - b * 7
        near_x = jnp.clip(x + a - 3, 0, 7)
        near_y = jnp.clip(y + b - 3, 0, 7)
        near_z = jnp.clip(z + dz - 3, 0, LANES - 1)
        near = near_x * 8 + near_y
        index = (near + (dz & 1) * ROWS, near + (1 - (dz & 1)) * ROWS)
        own = cell >> 7
        centre = (own + ROWS, own)
        d = dz >> 1
        low, first, third = d < 2, d < 1, d < 3
        left = lane_step < ROWS
        both, third_of, colour_of = [], [], []
        for k in range(4):
            at = pl.ds(k * SLOTS, STEP)
            even = [window[0, at, p * LANES : (p + 1) * LANES] for p in range(2)]
            odd = [window[1, at, p * LANES : (p + 1) * LANES] for p in range(2)] if k < 3 else even
            x_whole = jnp.where(left, even[0], odd[0]).astype(jnp.int32)
            y_whole = jnp.where(left, even[1], odd[1]).astype(jnp.int32)
            both.append((x_whole << 16) | y_whole)
            third_of.append(jnp.where(left, odd[0], even[0]))
            colour_of.append(jnp.where(left, odd[1], even[1]))

        def pick(tabs, swapped):
            got = [lane_take(t, index[swapped]) for t in tabs]
            value = jnp.where(
                low, jnp.where(first, got[0], got[1]), jnp.where(third, got[2], got[3])
            )
            return value, lane_take(tabs[1], centre[swapped])

        at_near, at_own = pick(both, 0)
        z_near, z_own = pick(third_of, 1)
        c_near, c_own = pick(colour_of, 1)
        diff = (
            ((at_near >> 16) - (at_own >> 16)).astype(jnp.float32) * (1.0 / SCALE),
            ((at_near & 65535) - (at_own & 65535)).astype(jnp.float32) * (1.0 / SCALE),
            z_near - z_own,
            c_near - c_own,
        )
        ox = (near_x - x).astype(jnp.float32) + diff[0]
        oy = (near_y - y).astype(jnp.float32) + diff[1]
        oz = (near_z - z).astype(jnp.float32) + diff[2]
        w = diff[3] * jnp.exp(-(ox * ox + oy * oy + oz * oz) / SMOOTH_SQ)
        wx, wy, wz = w * ox, w * oy, w * oz
        terms = (w, wx, wy, wz, wx * ox, wy * oy, wz * oz, wx * oy, wx * oz, wy * oz)
        out = jnp.zeros((STEP, LANES), jnp.float32)
        for q, term in enumerate(terms):
            out = jnp.where(lane_step == q, jnp.sum(term, axis=1, keepdims=True), out)
        moments[rows, :] = out
        return carry

    moments[SLOTS:, :] = jnp.zeros((2 * LANES - SLOTS, LANES), jnp.float32)
    group(0, 0)

    sums = jnp.concatenate([moments[0:LANES, :].T, moments[LANES:, :].T], axis=1)
    kappa = final_curvature(*[sums[q : q + 1, :] for q in range(10)])
    slot = lax.broadcasted_iota(jnp.int32, (1, 2 * LANES), 1)
    kappa = jnp.where(slot < counts_ref[0, 0], kappa, 0.0)
    kappa_ref[0] = kappa[:, :SLOTS]

    sub = lax.broadcasted_iota(jnp.int32, (ROWS, 2 * LANES), 0)
    spread = jnp.where(sub == (cells_row >> 7), SIGMA * kappa, 0.0)
    added = jnp.zeros((ROWS, LANES), jnp.float32)
    for piece in pieces(spread):
        added = added + jnp.dot(
            piece[:, :LANES], hot[1, SLOTS : SLOTS + LANES, :LANES], preferred_element_type=jnp.float32
        )
        added = added + jnp.dot(
            piece[:, LANES:SLOTS], hot[1, SLOTS + LANES : 2 * SLOTS, :LANES], preferred_element_type=jnp.float32
        )
    rhs = source_ref[...] + added.reshape(8, 8, LANES)
    rhs_ref[...] = rhs
    even = lax.rem(lax.axis_index("gx"), 2) == 0
    pressure = own_ref[...]

    def send(ref, high):
        ref[0:3] = jnp.where(high, pressure[5:8], pressure[0:3])
        ref[3:5] = jnp.where(high, rhs[6:8], rhs[0:2])

    send(even_ref, even)
    send(odd_ref, jnp.logical_not(even))


def curvature_call(*values):
    tile = jax.ShapeDtypeStruct((8, 8, LANES), jnp.float32)
    slab = jax.ShapeDtypeStruct((5, 8, LANES), jnp.float32)
    vmem = pl.BlockSpec(memory_space=pltpu.VMEM)
    hbm = pl.BlockSpec(memory_space=pltpu.HBM)
    smem = pl.BlockSpec(memory_space=pltpu.SMEM)
    return pl.pallas_call(
        curvature_kernel,
        out_shape=(jax.ShapeDtypeStruct((1, 1, SLOTS), jnp.float32), tile, tile, slab, slab),
        in_specs=[hbm] * 4 + [smem] + [hbm] * 2,
        out_specs=(vmem,) * 5,
        scratch_shapes=[
            pltpu.VMEM((3, 8, 8, LANES), jnp.float32),
            pltpu.VMEM((8, 8, LANES), jnp.float32),
            pltpu.VMEM((1, 1, SLOTS), jnp.int32),
            pltpu.VMEM((1, 1, SLOTS, LANES), jnp.int32),
            pltpu.VMEM((8, 8, LANES), jnp.float32),
            pltpu.SemaphoreType.DMA((6,)),
            pltpu.VMEM((2, 4 * ROWS, 3 * LANES), jnp.bfloat16),
            pltpu.VMEM((2, 4 * SLOTS, 3 * LANES), jnp.bfloat16),
            pltpu.VMEM((2, 4 * SLOTS, 4 * ROWS), jnp.float32),
            pltpu.VMEM((SLOTS, LANES), jnp.int32),
            pltpu.VMEM((8, 2 * LANES), jnp.int32),
            pltpu.VMEM((2 * LANES, LANES), jnp.float32),
        ],
        compiler_params=pltpu.CompilerParams(vmem_limit_bytes=16 * 2**20),
        name="curvature",
    )(*values)


def sides(first, second, even):
    return jnp.where(even, second, first), jnp.where(even, first, second)


CORNERS = (
    (False, 1, 0), (False, 2, 0), (False, 2, 1), (False, 4, 0),
    (True, 0, 0), (True, 0, 1), (True, 3, 0), (True, 1, 0),
)


def edges_kernel(pressure_ref, rhs_ref, xe_ref, xo_ref, even_ref, odd_ref):
    odd_x = lax.rem(lax.axis_index("gx"), 2)
    even_y = lax.rem(lax.axis_index("gy"), 2) == 0

    def send(tile, rows, high, low):
        even_ref[tile, rows] = jnp.where(even_y, high, low)
        odd_ref[tile, rows] = jnp.where(even_y, low, high)

    for tile in range(5):
        ref, away = (pressure_ref, tile) if tile < 3 else (rhs_ref, tile - 3)
        send(tile, slice(0, 8), ref[:, 7 - away, :], ref[:, away, :])
    for at, (above, tile, away) in enumerate(CORNERS):
        ends = []
        for row in (7 - away, away):
            pair = (xe_ref[1 - odd_x, tile, row : row + 1, :], xo_ref[tile, row : row + 1, :])
            ends.append(sides(*pair, odd_x == 0)[int(above)])
        send(5, slice(at, at + 1), *ends)


def edges_call(pressure, rhs, xe, xo):
    vmem = pl.BlockSpec(memory_space=pltpu.VMEM)
    strip = jax.ShapeDtypeStruct((6, 8, LANES), jnp.float32)
    return pl.pallas_call(
        edges_kernel,
        out_shape=(strip, strip),
        in_specs=[vmem] * 4,
        out_specs=(vmem, vmem),
        compiler_params=pltpu.CompilerParams(vmem_limit_bytes=8 * 2**20),
        name="edges",
    )(pressure, rhs, xe, xo)


def sweeps_kernel(
    n_gx, n_gy, kappa_ref, pressure_ref, rhs_ref, xe_ref, xo_ref, ye_ref, yo_ref,
    out_ref, curvature_ref, wide, source,
):
    at_x, at_y = lax.axis_index("gx"), lax.axis_index("gy")
    odd_x, odd_y = lax.rem(at_x, 2), lax.rem(at_y, 2)
    below, above = sides(xe_ref[1 - odd_x], xo_ref[...], odd_x == 0)
    left, right = sides(ye_ref[1 - odd_y], yo_ref[...], odd_y == 0)
    curvature_ref[...] = kappa_ref[...]
    wide[:, 8:, :] = jnp.zeros((14, 8, LANES), jnp.float32)
    source[:, 8:, :] = jnp.zeros((12, 8, LANES), jnp.float32)
    wide[0:3, 0:8, :], wide[3:11, 0:8, :], wide[11:14, 0:8, :] = below[0:3], pressure_ref[...], above[0:3]
    source[0:2, 0:8, :], source[2:10, 0:8, :], source[10:12, 0:8, :] = below[3:5], rhs_ref[...], above[3:5]
    for part, rows in ((right, (8, 9, 10)), (left, (15, 14, 13))):
        for tile in range(3):
            wide[3:11, rows[tile], :] = part[tile]
        for tile in range(2):
            source[2:10, rows[tile], :] = part[3 + tile]
        for at, (high, tile, away) in enumerate(CORNERS):
            row = rows[away]
            if tile < 3:
                plane = 11 + tile if high else tile
                wide[plane, row : row + 1, :] = part[5, at : at + 1]
            else:
                plane = 10 + tile - 3 if high else tile - 3
                source[plane, row : row + 1, :] = part[5, at : at + 1]
    current, rhs = wide[...], source[...]
    lane = lax.broadcasted_iota(jnp.int32, (1, 16, LANES), 2)
    sub = lax.broadcasted_iota(jnp.int32, (1, 16, LANES), 1)
    inside = (sub < jnp.where(at_y < n_gy - 1, 12, 8)) | (sub >= jnp.where(at_y > 0, 12, 16))
    for sweep in range(3):
        mid = current[1:-1]
        beside = current[2:] + current[:-2]
        beside = beside + pltpu.roll(mid, 15, 1) + pltpu.roll(mid, 1, 1)
        beside = beside + jnp.where(lane < LANES - 1, pltpu.roll(mid, LANES - 1, 2), 0.0)
        beside = beside + jnp.where(lane > 0, pltpu.roll(mid, 1, 2), 0.0)
        current = (beside + rhs[sweep : 12 - sweep]) / 6.0
        if sweep < 2:
            count = 12 - 2 * sweep
            plane = lax.broadcasted_iota(jnp.int32, (count, 1, 1), 0) + (sweep - 2)
            held = (plane >= jnp.where(at_x > 0, -2, 0)) & (plane < jnp.where(at_x < n_gx - 1, 10, 8))
            current = jnp.where(held & inside, current, 0.0)
    out_ref[...] = current[:, 0:8, :]


def sweeps_call(n_gx, n_gy, *values):
    vmem = pl.BlockSpec(memory_space=pltpu.VMEM)
    return pl.pallas_call(
        functools.partial(sweeps_kernel, n_gx, n_gy),
        out_shape=(
            jax.ShapeDtypeStruct((8, 8, LANES), jnp.float32),
            jax.ShapeDtypeStruct((1, 1, SLOTS), jnp.float32),
        ),
        in_specs=[vmem] * 7,
        out_specs=(vmem, vmem),
        scratch_shapes=[
            pltpu.VMEM((14, 16, LANES), jnp.float32),
            pltpu.VMEM((12, 16, LANES), jnp.float32),
        ],
        compiler_params=pltpu.CompilerParams(vmem_limit_bytes=8 * 2**20),
        name="sweeps",
    )(*values)


def swap_odd(value, axis):
    pairs = []
    for i in range(1, lax.axis_size(axis) - 1, 2):
        pairs += [(i, i + 1), (i + 1, i)]
    return lax.ppermute(value, axis, pairs)


def gather_even(value, axis):
    groups = [[i, i + 1] for i in range(0, lax.axis_size(axis), 2)]
    return lax.all_gather(value, axis, axis=0, axis_index_groups=groups)


def held(value):
    return pltpu.with_memory_space_constraint(value, pltpu.HBM)


def per_device(jitter, colour, surface_cells, neighbours, counts, pressure, source):
    kappa, own, rhs, even, odd = curvature_call(
        held(jitter), held(colour), held(surface_cells), held(neighbours),
        counts, held(source), held(pressure),
    )
    xo, xe = swap_odd(odd, "gx"), gather_even(even, "gx")
    even, odd = edges_call(own, rhs, xe, xo)
    yo, ye = swap_odd(odd, "gy"), gather_even(even, "gy")
    return sweeps_call(
        lax.axis_size("gx"), lax.axis_size("gy"), kappa, own, rhs, xe, xo, ye, yo
    )


def solution(mesh):
    placed = (
        P(None, "gx", "gy", None),
        P("gx", "gy", None),
        P("gx", "gy", None),
        P("gx", "gy", None, None),
        P("gx", "gy"),
        P("gx", "gy", None),
        P("gx", "gy", None),
    )
    return jax.shard_map(
        per_device,
        mesh=mesh,
        in_specs=placed,
        out_specs=(P("gx", "gy", None), P("gx", "gy", None)),
        check_vma=False,
    )
```

```python
import functools

import jax
import jax.numpy as jnp
from jax import lax
from jax.experimental import pallas as pl
from jax.experimental.pallas import tpu as pltpu
from jax.sharding import PartitionSpec as P

SIGMA = 1.0
SMOOTH_SQ = 4.0
SLOTS = 192
LANES = 128
ROWS = 64
FEW = 64
SCALE = 32767.0 / 0.3


def pieces(value):
    high = value.astype(jnp.bfloat16)
    rest = value - high.astype(jnp.float32)
    mid = rest.astype(jnp.bfloat16)
    low = (rest - mid.astype(jnp.float32)).astype(jnp.bfloat16)
    return high, mid, low


def lane_take(table, index):
    return jnp.take_along_axis(table, index, axis=1, mode="promise_in_bounds")


def final_curvature(total, gx, gy, gz, xx, yy, zz, xy, xz, yz):
    first = -2.0 / SMOOTH_SQ
    second = 4.0 / (SMOOTH_SQ * SMOOTH_SQ)
    gx, gy, gz = first * gx, first * gy, first * gz
    xx = second * xx + first * total
    yy = second * yy + first * total
    zz = second * zz + first * total
    xy, xz, yz = second * xy, second * xz, second * yz
    trace = xx + yy + zz
    quad = gx * gx * xx + gy * gy * yy + gz * gz * zz
    quad = quad + 2.0 * (gx * gy * xy + gx * gz * xz + gy * gz * yz)
    denom = 1.0 + gx * gx + gy * gy + gz * gz
    return -(trace - quad / denom) / jnp.sqrt(denom)


def curvature_of(size, count, codes_ref, kappa_ref, table, hot, window, place, row, moments, added):
    contract = (((1,), (1,)), ((), ()))
    width = -(-size // LANES) * LANES

    for parity, steps in ((0, 4), (1, 3)):
        starts = [k * SLOTS for k in range(steps)]
        some = [hot[parity, at : at + size] for at in starts]
        window[parity, : steps * size] = lax.dot_general(
            jnp.concatenate(some, axis=0), table[parity], contract,
            preferred_element_type=jnp.float32,
        )

    lane_step = lax.broadcasted_iota(jnp.int32, (size, LANES), 1)

    def group():
        rows = slice(0, size)
        cell = place[rows, :]
        code = codes_ref[0, 0, rows, :]
        x, y, z = cell >> 10, (cell >> 7) & 7, cell & 127
        a = (code * 1338) >> 16
        rest = code - a * 49
        b = (rest * 9363) >> 16
        dz = rest - b * 7
        near_x = jnp.clip(x + a - 3, 0, 7)
        near_y = jnp.clip(y + b - 3, 0, 7)
        near_z = jnp.clip(z + dz - 3, 0, LANES - 1)
        near = near_x * 8 + near_y
        index = (near + (dz & 1) * ROWS, near + (1 - (dz & 1)) * ROWS)
        own = cell >> 7
        centre = (own + ROWS, own)
        d = dz >> 1
        low, first, third = d < 2, d < 1, d < 3
        left = lane_step < ROWS
        both, third_of, colour_of = [], [], []
        for k in range(4):
            at = slice(k * size, (k + 1) * size)
            even = [window[0, at, p * LANES : (p + 1) * LANES] for p in range(2)]
            odd = [window[1, at, p * LANES : (p + 1) * LANES] for p in range(2)] if k < 3 else even
            x_whole = jnp.where(left, even[0], odd[0]).astype(jnp.int32)
            y_whole = jnp.where(left, even[1], odd[1]).astype(jnp.int32)
            both.append((x_whole << 16) | y_whole)
            third_of.append(jnp.where(left, odd[0], even[0]))
            colour_of.append(jnp.where(left, odd[1], even[1]))

        def pick(tabs, swapped):
            got = [lane_take(t, index[swapped]) for t in tabs]
            value = jnp.where(
                low, jnp.where(first, got[0], got[1]), jnp.where(third, got[2], got[3])
            )
            return value, lane_take(tabs[1], centre[swapped])

        at_near, at_own = pick(both, 0)
        z_near, z_own = pick(third_of, 1)
        c_near, c_own = pick(colour_of, 1)
        diff = (
            ((at_near >> 16) - (at_own >> 16)).astype(jnp.float32) * (1.0 / SCALE),
            ((at_near & 65535) - (at_own & 65535)).astype(jnp.float32) * (1.0 / SCALE),
            z_near - z_own,
            c_near - c_own,
        )
        ox = (near_x - x).astype(jnp.float32) + diff[0]
        oy = (near_y - y).astype(jnp.float32) + diff[1]
        oz = (near_z - z).astype(jnp.float32) + diff[2]
        w = diff[3] * jnp.exp(-(ox * ox + oy * oy + oz * oz) / SMOOTH_SQ)
        wx, wy, wz = w * ox, w * oy, w * oz
        terms = (w, wx, wy, wz, wx * ox, wy * oy, wz * oz, wx * oy, wx * oz, wy * oz)
        out = jnp.zeros((size, LANES), jnp.float32)
        for q, term in enumerate(terms):
            out = jnp.where(lane_step == q, jnp.sum(term, axis=1, keepdims=True), out)
        moments[rows, :] = out

    moments[size:width, :] = jnp.zeros((width - size, LANES), jnp.float32)
    group()

    blocks = [slice(at, at + LANES) for at in range(0, width, LANES)]
    sums = jnp.concatenate([moments[block, :].T for block in blocks], axis=1)
    kappa = final_curvature(*[sums[q : q + 1, :] for q in range(10)])
    slot = lax.broadcasted_iota(jnp.int32, (1, width), 1)
    kappa = jnp.where(slot < count, kappa, 0.0)
    whole = jnp.concatenate([kappa, jnp.zeros((1, 2 * LANES), jnp.float32)], axis=1)
    kappa_ref[0] = whole[:, :SLOTS]

    sub = lax.broadcasted_iota(jnp.int32, (ROWS, width), 0)
    spread = jnp.where(sub == (row[0:1, :width] >> 7), SIGMA * kappa, 0.0)
    total = jnp.zeros((ROWS, LANES), jnp.float32)
    for piece in pieces(spread):
        for block in blocks:
            end = min(block.stop, SLOTS)
            total = total + jnp.dot(
                piece[:, block.start : end],
                hot[1, SLOTS + block.start : SLOTS + end, :LANES],
                preferred_element_type=jnp.float32,
            )
    added[...] = total


def curvature_kernel(
    jitter_hbm, colour_hbm, cells_hbm, codes_hbm, counts_ref, source_hbm, pressure_hbm,
    kappa_ref, own_ref, rhs_ref, even_ref, odd_ref,
    jitter_ref, colour_ref, cells_ref, codes_ref, source_ref, arrived,
    table, hot, window, place, row, moments, added,
):
    copies = [
        pltpu.make_async_copy(source, target, arrived.at[i])
        for i, (source, target) in enumerate((
            (cells_hbm, cells_ref),
            (jitter_hbm, jitter_ref),
            (colour_hbm, colour_ref),
            (codes_hbm, codes_ref),
            (source_hbm, source_ref),
            (pressure_hbm, own_ref),
        ))
    ]
    for copy in copies:
        copy.start()

    copies[0].wait()
    row[...] = jnp.zeros_like(row)
    row[0:1, 0:SLOTS] = cells_ref[0]
    cells_row = row[0:1, :]
    as_float = cells_row.astype(jnp.float32)
    for h in range(2):
        part = jnp.broadcast_to(as_float[:, h * LANES : (h + 1) * LANES], (LANES, LANES))
        turned = part.T.astype(jnp.int32)
        keep = min(LANES, SLOTS - h * LANES)
        place[h * LANES : h * LANES + keep, :] = turned[:keep]

    lane = lax.broadcasted_iota(jnp.int32, (SLOTS, LANES), 1)
    z_of = place[...] & 127
    for step in range(7):
        target = jnp.clip(z_of + (step - 3), 0, LANES - 1)
        one = jnp.where(lane == target, 1.0, 0.0).astype(jnp.bfloat16)
        for q in range(3):
            hot[step % 2, (step // 2) * SLOTS : (step // 2 + 1) * SLOTS, q * LANES : (q + 1) * LANES] = one

    for copy in copies[1:]:
        copy.wait()
    whole_x = jnp.round(jitter_ref[0] * SCALE)
    whole_y = jnp.round(jitter_ref[1] * SCALE) + 32768.0
    for c, value in enumerate((whole_x, jitter_ref[2], whole_y, colour_ref[...])):
        for q, piece in enumerate(pieces(value.reshape(ROWS, LANES))):
            columns = slice(q * LANES, (q + 1) * LANES)
            table[0, c * ROWS : (c + 1) * ROWS, columns] = piece
            table[1, (c ^ 1) * ROWS : ((c ^ 1) + 1) * ROWS, columns] = piece

    count = counts_ref[0, 0]
    rest = (codes_ref, kappa_ref, table, hot, window, place, row, moments, added)
    pl.when(count <= FEW)(lambda: curvature_of(FEW, count, *rest))
    pl.when(count > FEW)(lambda: curvature_of(SLOTS, count, *rest))

    rhs = source_ref[...] + added[...].reshape(8, 8, LANES)
    rhs_ref[...] = rhs
    even = lax.rem(lax.axis_index("gx"), 2) == 0
    pressure = own_ref[...]

    def send(ref, high):
        ref[0:3] = jnp.where(high, pressure[5:8], pressure[0:3])
        ref[3:5] = jnp.where(high, rhs[6:8], rhs[0:2])

    send(even_ref, even)
    send(odd_ref, jnp.logical_not(even))


def curvature_call(*values):
    tile = jax.ShapeDtypeStruct((8, 8, LANES), jnp.float32)
    slab = jax.ShapeDtypeStruct((5, 8, LANES), jnp.float32)
    vmem = pl.BlockSpec(memory_space=pltpu.VMEM)
    hbm = pl.BlockSpec(memory_space=pltpu.HBM)
    smem = pl.BlockSpec(memory_space=pltpu.SMEM)
    return pl.pallas_call(
        curvature_kernel,
        out_shape=(jax.ShapeDtypeStruct((1, 1, SLOTS), jnp.float32), tile, tile, slab, slab),
        in_specs=[hbm] * 4 + [smem] + [hbm] * 2,
        out_specs=(vmem,) * 5,
        scratch_shapes=[
            pltpu.VMEM((3, 8, 8, LANES), jnp.float32),
            pltpu.VMEM((8, 8, LANES), jnp.float32),
            pltpu.VMEM((1, 1, SLOTS), jnp.int32),
            pltpu.VMEM((1, 1, SLOTS, LANES), jnp.int32),
            pltpu.VMEM((8, 8, LANES), jnp.float32),
            pltpu.SemaphoreType.DMA((6,)),
            pltpu.VMEM((2, 4 * ROWS, 3 * LANES), jnp.bfloat16),
            pltpu.VMEM((2, 4 * SLOTS, 3 * LANES), jnp.bfloat16),
            pltpu.VMEM((2, 4 * SLOTS, 4 * ROWS), jnp.float32),
            pltpu.VMEM((SLOTS, LANES), jnp.int32),
            pltpu.VMEM((8, 2 * LANES), jnp.int32),
            pltpu.VMEM((2 * LANES, LANES), jnp.float32),
            pltpu.VMEM((ROWS, LANES), jnp.float32),
        ],
        compiler_params=pltpu.CompilerParams(vmem_limit_bytes=16 * 2**20),
        name="curvature",
    )(*values)


def sides(first, second, even):
    return jnp.where(even, second, first), jnp.where(even, first, second)


CORNERS = (
    (False, 1, 0), (False, 2, 0), (False, 2, 1), (False, 4, 0),
    (True, 0, 0), (True, 0, 1), (True, 3, 0), (True, 1, 0),
)


def edges_kernel(pressure_ref, rhs_ref, xe_ref, xo_ref, even_ref, odd_ref):
    odd_x = lax.rem(lax.axis_index("gx"), 2)
    even_y = lax.rem(lax.axis_index("gy"), 2) == 0

    def send(tile, rows, high, low):
        even_ref[tile, rows] = jnp.where(even_y, high, low)
        odd_ref[tile, rows] = jnp.where(even_y, low, high)

    for tile in range(5):
        ref, away = (pressure_ref, tile) if tile < 3 else (rhs_ref, tile - 3)
        send(tile, slice(0, 8), ref[:, 7 - away, :], ref[:, away, :])
    for at, (above, tile, away) in enumerate(CORNERS):
        ends = []
        for row in (7 - away, away):
            pair = (xe_ref[1 - odd_x, tile, row : row + 1, :], xo_ref[tile, row : row + 1, :])
            ends.append(sides(*pair, odd_x == 0)[int(above)])
        send(5, slice(at, at + 1), *ends)


def edges_call(pressure, rhs, xe, xo):
    vmem = pl.BlockSpec(memory_space=pltpu.VMEM)
    strip = jax.ShapeDtypeStruct((6, 8, LANES), jnp.float32)
    return pl.pallas_call(
        edges_kernel,
        out_shape=(strip, strip),
        in_specs=[vmem] * 4,
        out_specs=(vmem, vmem),
        compiler_params=pltpu.CompilerParams(vmem_limit_bytes=8 * 2**20),
        name="edges",
    )(pressure, rhs, xe, xo)


def sweeps_kernel(
    n_gx, n_gy, kappa_ref, pressure_ref, rhs_ref, xe_ref, xo_ref, ye_ref, yo_ref,
    out_ref, curvature_ref, wide, source,
):
    at_x, at_y = lax.axis_index("gx"), lax.axis_index("gy")
    odd_x, odd_y = lax.rem(at_x, 2), lax.rem(at_y, 2)
    below, above = sides(xe_ref[1 - odd_x], xo_ref[...], odd_x == 0)
    left, right = sides(ye_ref[1 - odd_y], yo_ref[...], odd_y == 0)
    curvature_ref[...] = kappa_ref[...]
    wide[:, 8:, :] = jnp.zeros((14, 8, LANES), jnp.float32)
    source[:, 8:, :] = jnp.zeros((12, 8, LANES), jnp.float32)
    wide[0:3, 0:8, :], wide[3:11, 0:8, :], wide[11:14, 0:8, :] = below[0:3], pressure_ref[...], above[0:3]
    source[0:2, 0:8, :], source[2:10, 0:8, :], source[10:12, 0:8, :] = below[3:5], rhs_ref[...], above[3:5]
    for part, rows in ((right, (8, 9, 10)), (left, (15, 14, 13))):
        for tile in range(3):
            wide[3:11, rows[tile], :] = part[tile]
        for tile in range(2):
            source[2:10, rows[tile], :] = part[3 + tile]
        for at, (high, tile, away) in enumerate(CORNERS):
            row = rows[away]
            if tile < 3:
                plane = 11 + tile if high else tile
                wide[plane, row : row + 1, :] = part[5, at : at + 1]
            else:
                plane = 10 + tile - 3 if high else tile - 3
                source[plane, row : row + 1, :] = part[5, at : at + 1]
    current, rhs = wide[...], source[...]
    lane = lax.broadcasted_iota(jnp.int32, (1, 16, LANES), 2)
    sub = lax.broadcasted_iota(jnp.int32, (1, 16, LANES), 1)
    inside = (sub < jnp.where(at_y < n_gy - 1, 12, 8)) | (sub >= jnp.where(at_y > 0, 12, 16))
    for sweep in range(3):
        mid = current[1:-1]
        beside = current[2:] + current[:-2]
        beside = beside + pltpu.roll(mid, 15, 1) + pltpu.roll(mid, 1, 1)
        beside = beside + jnp.where(lane < LANES - 1, pltpu.roll(mid, LANES - 1, 2), 0.0)
        beside = beside + jnp.where(lane > 0, pltpu.roll(mid, 1, 2), 0.0)
        current = (beside + rhs[sweep : 12 - sweep]) / 6.0
        if sweep < 2:
            count = 12 - 2 * sweep
            plane = lax.broadcasted_iota(jnp.int32, (count, 1, 1), 0) + (sweep - 2)
            held = (plane >= jnp.where(at_x > 0, -2, 0)) & (plane < jnp.where(at_x < n_gx - 1, 10, 8))
            current = jnp.where(held & inside, current, 0.0)
    out_ref[...] = current[:, 0:8, :]


def sweeps_call(n_gx, n_gy, *values):
    vmem = pl.BlockSpec(memory_space=pltpu.VMEM)
    return pl.pallas_call(
        functools.partial(sweeps_kernel, n_gx, n_gy),
        out_shape=(
            jax.ShapeDtypeStruct((8, 8, LANES), jnp.float32),
            jax.ShapeDtypeStruct((1, 1, SLOTS), jnp.float32),
        ),
        in_specs=[vmem] * 7,
        out_specs=(vmem, vmem),
        scratch_shapes=[
            pltpu.VMEM((14, 16, LANES), jnp.float32),
            pltpu.VMEM((12, 16, LANES), jnp.float32),
        ],
        compiler_params=pltpu.CompilerParams(vmem_limit_bytes=8 * 2**20),
        name="sweeps",
    )(*values)


def swap_odd(value, axis):
    pairs = []
    for i in range(1, lax.axis_size(axis) - 1, 2):
        pairs += [(i, i + 1), (i + 1, i)]
    return lax.ppermute(value, axis, pairs)


def gather_even(value, axis):
    groups = [[i, i + 1] for i in range(0, lax.axis_size(axis), 2)]
    return lax.all_gather(value, axis, axis=0, axis_index_groups=groups)


def held(value):
    return pltpu.with_memory_space_constraint(value, pltpu.HBM)


def per_device(jitter, colour, surface_cells, neighbours, counts, pressure, source):
    kappa, own, rhs, even, odd = curvature_call(
        held(jitter), held(colour), held(surface_cells), held(neighbours),
        counts, held(source), held(pressure),
    )
    xo, xe = swap_odd(odd, "gx"), gather_even(even, "gx")
    even, odd = edges_call(own, rhs, xe, xo)
    yo, ye = swap_odd(odd, "gy"), gather_even(even, "gy")
    return sweeps_call(
        lax.axis_size("gx"), lax.axis_size("gy"), kappa, own, rhs, xe, xo, ye, yo
    )


def solution(mesh):
    placed = (
        P(None, "gx", "gy", None),
        P("gx", "gy", None),
        P("gx", "gy", None),
        P("gx", "gy", None, None),
        P("gx", "gy"),
        P("gx", "gy", None),
        P("gx", "gy", None),
    )
    return jax.shard_map(
        per_device,
        mesh=mesh,
        in_specs=placed,
        out_specs=(P("gx", "gy", None), P("gx", "gy", None)),
        check_vma=False,
    )
```

```python
import functools

import jax
import jax.numpy as jnp
from jax import lax
from jax.experimental import pallas as pl
from jax.experimental.pallas import tpu as pltpu
from jax.sharding import PartitionSpec as P

SIGMA = 1.0
SMOOTH_SQ = 4.0
SLOTS = 192
LANES = 128
ROWS = 64
SIZES = (32, 64)
SCALE = 32767.0 / 0.3


def pieces(value):
    high = value.astype(jnp.bfloat16)
    rest = value - high.astype(jnp.float32)
    mid = rest.astype(jnp.bfloat16)
    low = (rest - mid.astype(jnp.float32)).astype(jnp.bfloat16)
    return high, mid, low


def lane_take(table, index):
    return jnp.take_along_axis(table, index, axis=1, mode="promise_in_bounds")


def final_curvature(total, gx, gy, gz, xx, yy, zz, xy, xz, yz):
    first = -2.0 / SMOOTH_SQ
    second = 4.0 / (SMOOTH_SQ * SMOOTH_SQ)
    gx, gy, gz = first * gx, first * gy, first * gz
    xx = second * xx + first * total
    yy = second * yy + first * total
    zz = second * zz + first * total
    xy, xz, yz = second * xy, second * xz, second * yz
    trace = xx + yy + zz
    quad = gx * gx * xx + gy * gy * yy + gz * gz * zz
    quad = quad + 2.0 * (gx * gy * xy + gx * gz * xz + gy * gz * yz)
    denom = 1.0 + gx * gx + gy * gy + gz * gz
    return -(trace - quad / denom) / jnp.sqrt(denom)


def curvature_of(size, count, codes_ref, kappa_ref, table, hot, window, place, row, moments, added):
    contract = (((1,), (1,)), ((), ()))
    width = -(-size // LANES) * LANES

    for parity, steps in ((0, 4), (1, 3)):
        starts = [k * SLOTS for k in range(steps)]
        some = [hot[parity, at : at + size] for at in starts]
        window[parity, : steps * size] = lax.dot_general(
            jnp.concatenate(some, axis=0), table[parity], contract,
            preferred_element_type=jnp.float32,
        )

    lane_step = lax.broadcasted_iota(jnp.int32, (size, LANES), 1)

    def group():
        rows = slice(0, size)
        cell = place[rows, :]
        code = codes_ref[0, 0, rows, :]
        x, y, z = cell >> 10, (cell >> 7) & 7, cell & 127
        a = (code * 1338) >> 16
        rest = code - a * 49
        b = (rest * 9363) >> 16
        dz = rest - b * 7
        near_x = jnp.clip(x + a - 3, 0, 7)
        near_y = jnp.clip(y + b - 3, 0, 7)
        near_z = jnp.clip(z + dz - 3, 0, LANES - 1)
        near = near_x * 8 + near_y
        index = (near + (dz & 1) * ROWS, near + (1 - (dz & 1)) * ROWS)
        own = cell >> 7
        centre = (own + ROWS, own)
        d = dz >> 1
        low, first, third = d < 2, d < 1, d < 3
        left = lane_step < ROWS
        both, third_of, colour_of = [], [], []
        for k in range(4):
            at = slice(k * size, (k + 1) * size)
            even = [window[0, at, p * LANES : (p + 1) * LANES] for p in range(2)]
            odd = [window[1, at, p * LANES : (p + 1) * LANES] for p in range(2)] if k < 3 else even
            x_whole = jnp.where(left, even[0], odd[0]).astype(jnp.int32)
            y_whole = jnp.where(left, even[1], odd[1]).astype(jnp.int32)
            both.append((x_whole << 16) | y_whole)
            third_of.append(jnp.where(left, odd[0], even[0]))
            colour_of.append(jnp.where(left, odd[1], even[1]))

        def pick(tabs, swapped):
            got = [lane_take(t, index[swapped]) for t in tabs]
            value = jnp.where(
                low, jnp.where(first, got[0], got[1]), jnp.where(third, got[2], got[3])
            )
            return value, lane_take(tabs[1], centre[swapped])

        at_near, at_own = pick(both, 0)
        z_near, z_own = pick(third_of, 1)
        c_near, c_own = pick(colour_of, 1)
        diff = (
            ((at_near >> 16) - (at_own >> 16)).astype(jnp.float32) * (1.0 / SCALE),
            ((at_near & 65535) - (at_own & 65535)).astype(jnp.float32) * (1.0 / SCALE),
            z_near - z_own,
            c_near - c_own,
        )
        ox = (near_x - x).astype(jnp.float32) + diff[0]
        oy = (near_y - y).astype(jnp.float32) + diff[1]
        oz = (near_z - z).astype(jnp.float32) + diff[2]
        w = diff[3] * jnp.exp(-(ox * ox + oy * oy + oz * oz) / SMOOTH_SQ)
        wx, wy, wz = w * ox, w * oy, w * oz
        terms = (w, wx, wy, wz, wx * ox, wy * oy, wz * oz, wx * oy, wx * oz, wy * oz)
        return [jnp.sum(term, axis=1, keepdims=True) for term in terms]

    slot = lax.broadcasted_iota(jnp.int32, (size, 1), 0)
    kappa = jnp.where(slot < count, final_curvature(*group()), 0.0)

    sub = lax.broadcasted_iota(jnp.int32, (ROWS, width), 0)
    row_hot = jnp.where(sub == (row[0:1, :width] >> 7), 1.0, 0.0).astype(jnp.bfloat16)[:, :size]
    spread = jnp.where(lane_step == (place[0:size, :] & 127), SIGMA * kappa, 0.0)
    parts = jnp.dot(
        row_hot, jnp.concatenate(pieces(spread), axis=1), preferred_element_type=jnp.float32
    )
    added[...] = parts[:, :LANES] + parts[:, LANES : 2 * LANES] + parts[:, 2 * LANES :]

    moments[0:size, :] = jnp.broadcast_to(kappa, (size, LANES))
    moments[size:width, :] = jnp.zeros((width - size, LANES), jnp.float32)
    turned = [moments[at : at + LANES, :].T[0:1] for at in range(0, width, LANES)]
    turned = jnp.concatenate(turned + [jnp.zeros((1, 2 * LANES), jnp.float32)], axis=1)
    kappa_ref[0] = turned[:, :SLOTS]


def curvature_kernel(
    jitter_hbm, colour_hbm, cells_hbm, codes_hbm, counts_ref, source_hbm, pressure_hbm,
    kappa_ref, own_ref, rhs_ref, even_ref, odd_ref,
    jitter_ref, colour_ref, cells_ref, codes_ref, source_ref, arrived,
    table, hot, window, place, row, moments, added,
):
    copies = [
        pltpu.make_async_copy(source, target, arrived.at[i])
        for i, (source, target) in enumerate((
            (cells_hbm, cells_ref),
            (jitter_hbm, jitter_ref),
            (colour_hbm, colour_ref),
            (codes_hbm, codes_ref),
            (source_hbm, source_ref),
            (pressure_hbm, own_ref),
        ))
    ]
    for copy in copies:
        copy.start()

    copies[0].wait()
    row[...] = jnp.zeros_like(row)
    row[0:1, 0:SLOTS] = cells_ref[0]
    cells_row = row[0:1, :]
    as_float = cells_row.astype(jnp.float32)
    for h in range(2):
        part = jnp.broadcast_to(as_float[:, h * LANES : (h + 1) * LANES], (LANES, LANES))
        turned = part.T.astype(jnp.int32)
        keep = min(LANES, SLOTS - h * LANES)
        place[h * LANES : h * LANES + keep, :] = turned[:keep]

    lane = lax.broadcasted_iota(jnp.int32, (SLOTS, LANES), 1)
    z_of = place[...] & 127
    for step in range(7):
        target = jnp.clip(z_of + (step - 3), 0, LANES - 1)
        one = jnp.where(lane == target, 1.0, 0.0).astype(jnp.bfloat16)
        for q in range(3):
            hot[step % 2, (step // 2) * SLOTS : (step // 2 + 1) * SLOTS, q * LANES : (q + 1) * LANES] = one

    for copy in copies[1:]:
        copy.wait()
    whole_x = jnp.round(jitter_ref[0] * SCALE)
    whole_y = jnp.round(jitter_ref[1] * SCALE) + 32768.0
    for c, value in enumerate((whole_x, jitter_ref[2], whole_y, colour_ref[...])):
        for q, piece in enumerate(pieces(value.reshape(ROWS, LANES))):
            columns = slice(q * LANES, (q + 1) * LANES)
            table[0, c * ROWS : (c + 1) * ROWS, columns] = piece
            table[1, (c ^ 1) * ROWS : ((c ^ 1) + 1) * ROWS, columns] = piece

    count = counts_ref[0, 0]
    rest = (codes_ref, kappa_ref, table, hot, window, place, row, moments, added)
    pl.when(count <= SIZES[0])(lambda: curvature_of(SIZES[0], count, *rest))
    pl.when((count > SIZES[0]) & (count <= SIZES[1]))(lambda: curvature_of(SIZES[1], count, *rest))
    pl.when(count > SIZES[1])(lambda: curvature_of(SLOTS, count, *rest))

    rhs = source_ref[...] + added[...].reshape(8, 8, LANES)
    rhs_ref[...] = rhs
    even = lax.rem(lax.axis_index("gx"), 2) == 0
    pressure = own_ref[...]

    def send(ref, high):
        ref[0:3] = jnp.where(high, pressure[5:8], pressure[0:3])
        ref[3:5] = jnp.where(high, rhs[6:8], rhs[0:2])

    send(even_ref, even)
    send(odd_ref, jnp.logical_not(even))


def curvature_call(*values):
    tile = jax.ShapeDtypeStruct((8, 8, LANES), jnp.float32)
    slab = jax.ShapeDtypeStruct((5, 8, LANES), jnp.float32)
    vmem = pl.BlockSpec(memory_space=pltpu.VMEM)
    hbm = pl.BlockSpec(memory_space=pltpu.HBM)
    smem = pl.BlockSpec(memory_space=pltpu.SMEM)
    return pl.pallas_call(
        curvature_kernel,
        out_shape=(jax.ShapeDtypeStruct((1, 1, SLOTS), jnp.float32), tile, tile, slab, slab),
        in_specs=[hbm] * 4 + [smem] + [hbm] * 2,
        out_specs=(vmem,) * 5,
        scratch_shapes=[
            pltpu.VMEM((3, 8, 8, LANES), jnp.float32),
            pltpu.VMEM((8, 8, LANES), jnp.float32),
            pltpu.VMEM((1, 1, SLOTS), jnp.int32),
            pltpu.VMEM((1, 1, SLOTS, LANES), jnp.int32),
            pltpu.VMEM((8, 8, LANES), jnp.float32),
            pltpu.SemaphoreType.DMA((6,)),
            pltpu.VMEM((2, 4 * ROWS, 3 * LANES), jnp.bfloat16),
            pltpu.VMEM((2, 4 * SLOTS, 3 * LANES), jnp.bfloat16),
            pltpu.VMEM((2, 4 * SLOTS, 4 * ROWS), jnp.float32),
            pltpu.VMEM((SLOTS, LANES), jnp.int32),
            pltpu.VMEM((8, 2 * LANES), jnp.int32),
            pltpu.VMEM((2 * LANES, LANES), jnp.float32),
            pltpu.VMEM((ROWS, LANES), jnp.float32),
        ],
        compiler_params=pltpu.CompilerParams(vmem_limit_bytes=16 * 2**20),
        name="curvature",
    )(*values)


def sides(first, second, even):
    return jnp.where(even, second, first), jnp.where(even, first, second)


CORNERS = (
    (False, 1, 0), (False, 2, 0), (False, 2, 1), (False, 4, 0),
    (True, 0, 0), (True, 0, 1), (True, 3, 0), (True, 1, 0),
)


def edges_kernel(pressure_ref, rhs_ref, xe_ref, xo_ref, even_ref, odd_ref):
    odd_x = lax.rem(lax.axis_index("gx"), 2)
    even_y = lax.rem(lax.axis_index("gy"), 2) == 0

    def send(tile, rows, high, low):
        even_ref[tile, rows] = jnp.where(even_y, high, low)
        odd_ref[tile, rows] = jnp.where(even_y, low, high)

    for tile in range(5):
        ref, away = (pressure_ref, tile) if tile < 3 else (rhs_ref, tile - 3)
        send(tile, slice(0, 8), ref[:, 7 - away, :], ref[:, away, :])
    for at, (above, tile, away) in enumerate(CORNERS):
        ends = []
        for row in (7 - away, away):
            pair = (xe_ref[1 - odd_x, tile, row : row + 1, :], xo_ref[tile, row : row + 1, :])
            ends.append(sides(*pair, odd_x == 0)[int(above)])
        send(5, slice(at, at + 1), *ends)


def edges_call(pressure, rhs, xe, xo):
    vmem = pl.BlockSpec(memory_space=pltpu.VMEM)
    strip = jax.ShapeDtypeStruct((6, 8, LANES), jnp.float32)
    return pl.pallas_call(
        edges_kernel,
        out_shape=(strip, strip),
        in_specs=[vmem] * 4,
        out_specs=(vmem, vmem),
        compiler_params=pltpu.CompilerParams(vmem_limit_bytes=8 * 2**20),
        name="edges",
    )(pressure, rhs, xe, xo)


def sweeps_kernel(
    n_gx, n_gy, kappa_ref, pressure_ref, rhs_ref, xe_ref, xo_ref, ye_ref, yo_ref,
    out_ref, curvature_ref, wide, source,
):
    at_x, at_y = lax.axis_index("gx"), lax.axis_index("gy")
    odd_x, odd_y = lax.rem(at_x, 2), lax.rem(at_y, 2)
    below, above = sides(xe_ref[1 - odd_x], xo_ref[...], odd_x == 0)
    left, right = sides(ye_ref[1 - odd_y], yo_ref[...], odd_y == 0)
    curvature_ref[...] = kappa_ref[...]
    wide[:, 8:, :] = jnp.zeros((14, 8, LANES), jnp.float32)
    source[:, 8:, :] = jnp.zeros((12, 8, LANES), jnp.float32)
    wide[0:3, 0:8, :], wide[3:11, 0:8, :], wide[11:14, 0:8, :] = below[0:3], pressure_ref[...], above[0:3]
    source[0:2, 0:8, :], source[2:10, 0:8, :], source[10:12, 0:8, :] = below[3:5], rhs_ref[...], above[3:5]
    for part, rows in ((right, (8, 9, 10)), (left, (15, 14, 13))):
        for tile in range(3):
            wide[3:11, rows[tile], :] = part[tile]
        for tile in range(2):
            source[2:10, rows[tile], :] = part[3 + tile]
        for at, (high, tile, away) in enumerate(CORNERS):
            row = rows[away]
            if tile < 3:
                plane = 11 + tile if high else tile
                wide[plane, row : row + 1, :] = part[5, at : at + 1]
            else:
                plane = 10 + tile - 3 if high else tile - 3
                source[plane, row : row + 1, :] = part[5, at : at + 1]
    current, rhs = wide[...], source[...]
    lane = lax.broadcasted_iota(jnp.int32, (1, 16, LANES), 2)
    sub = lax.broadcasted_iota(jnp.int32, (1, 16, LANES), 1)
    inside = (sub < jnp.where(at_y < n_gy - 1, 12, 8)) | (sub >= jnp.where(at_y > 0, 12, 16))
    for sweep in range(3):
        mid = current[1:-1]
        beside = current[2:] + current[:-2]
        beside = beside + pltpu.roll(mid, 15, 1) + pltpu.roll(mid, 1, 1)
        beside = beside + jnp.where(lane < LANES - 1, pltpu.roll(mid, LANES - 1, 2), 0.0)
        beside = beside + jnp.where(lane > 0, pltpu.roll(mid, 1, 2), 0.0)
        current = (beside + rhs[sweep : 12 - sweep]) / 6.0
        if sweep < 2:
            count = 12 - 2 * sweep
            plane = lax.broadcasted_iota(jnp.int32, (count, 1, 1), 0) + (sweep - 2)
            held = (plane >= jnp.where(at_x > 0, -2, 0)) & (plane < jnp.where(at_x < n_gx - 1, 10, 8))
            current = jnp.where(held & inside, current, 0.0)
    out_ref[...] = current[:, 0:8, :]


def sweeps_call(n_gx, n_gy, *values):
    vmem = pl.BlockSpec(memory_space=pltpu.VMEM)
    return pl.pallas_call(
        functools.partial(sweeps_kernel, n_gx, n_gy),
        out_shape=(
            jax.ShapeDtypeStruct((8, 8, LANES), jnp.float32),
            jax.ShapeDtypeStruct((1, 1, SLOTS), jnp.float32),
        ),
        in_specs=[vmem] * 7,
        out_specs=(vmem, vmem),
        scratch_shapes=[
            pltpu.VMEM((14, 16, LANES), jnp.float32),
            pltpu.VMEM((12, 16, LANES), jnp.float32),
        ],
        compiler_params=pltpu.CompilerParams(vmem_limit_bytes=8 * 2**20),
        name="sweeps",
    )(*values)


def swap_odd(value, axis):
    pairs = []
    for i in range(1, lax.axis_size(axis) - 1, 2):
        pairs += [(i, i + 1), (i + 1, i)]
    return lax.ppermute(value, axis, pairs)


def gather_even(value, axis):
    groups = [[i, i + 1] for i in range(0, lax.axis_size(axis), 2)]
    return lax.all_gather(value, axis, axis=0, axis_index_groups=groups)


def held(value):
    return pltpu.with_memory_space_constraint(value, pltpu.HBM)


def per_device(jitter, colour, surface_cells, neighbours, counts, pressure, source):
    kappa, own, rhs, even, odd = curvature_call(
        held(jitter), held(colour), held(surface_cells), held(neighbours),
        counts, held(source), held(pressure),
    )
    xo, xe = swap_odd(odd, "gx"), gather_even(even, "gx")
    even, odd = edges_call(own, rhs, xe, xo)
    yo, ye = swap_odd(odd, "gy"), gather_even(even, "gy")
    return sweeps_call(
        lax.axis_size("gx"), lax.axis_size("gy"), kappa, own, rhs, xe, xo, ye, yo
    )


def solution(mesh):
    placed = (
        P(None, "gx", "gy", None),
        P("gx", "gy", None),
        P("gx", "gy", None),
        P("gx", "gy", None, None),
        P("gx", "gy"),
        P("gx", "gy", None),
        P("gx", "gy", None),
    )
    return jax.shard_map(
        per_device,
        mesh=mesh,
        in_specs=placed,
        out_specs=(P("gx", "gy", None), P("gx", "gy", None)),
        check_vma=False,
    )
```

```python
import functools

import jax
import jax.numpy as jnp
from jax import lax
from jax.experimental import pallas as pl
from jax.experimental.pallas import tpu as pltpu
from jax.sharding import PartitionSpec as P

SIGMA = 1.0
SMOOTH_SQ = 4.0
SLOTS = 192
LANES = 128
ROWS = 64
SIZES = (32, 64)
SCALE = 32767.0 / 0.3


def pieces(value):
    high = value.astype(jnp.bfloat16)
    rest = value - high.astype(jnp.float32)
    mid = rest.astype(jnp.bfloat16)
    low = (rest - mid.astype(jnp.float32)).astype(jnp.bfloat16)
    return high, mid, low


def lane_take(table, index):
    return jnp.take_along_axis(table, index, axis=1, mode="promise_in_bounds")


def final_curvature(total, gx, gy, gz, xx, yy, zz, xy, xz, yz):
    first = -2.0 / SMOOTH_SQ
    second = 4.0 / (SMOOTH_SQ * SMOOTH_SQ)
    gx, gy, gz = first * gx, first * gy, first * gz
    xx = second * xx + first * total
    yy = second * yy + first * total
    zz = second * zz + first * total
    xy, xz, yz = second * xy, second * xz, second * yz
    trace = xx + yy + zz
    quad = gx * gx * xx + gy * gy * yy + gz * gz * zz
    quad = quad + 2.0 * (gx * gy * xy + gx * gz * xz + gy * gz * yz)
    denom = 1.0 + gx * gx + gy * gy + gz * gz
    return -(trace - quad / denom) / jnp.sqrt(denom)


def curvature_of(size, count, codes_ref, kappa_ref, table, hot, window, place, row, moments, added):
    contract = (((1,), (1,)), ((), ()))
    width = -(-size // LANES) * LANES

    for parity, steps in ((0, 4), (1, 3)):
        starts = [k * SLOTS for k in range(steps)]
        some = [hot[parity, at : at + size] for at in starts]
        window[parity, : steps * size] = lax.dot_general(
            jnp.concatenate(some, axis=0), table[parity], contract,
            preferred_element_type=jnp.float32,
        )

    lane_step = lax.broadcasted_iota(jnp.int32, (size, LANES), 1)

    def group():
        rows = slice(0, size)
        cell = place[rows, :]
        code = codes_ref[0, 0, rows, :]
        x, y, z = cell >> 10, (cell >> 7) & 7, cell & 127
        a = (code * 1338) >> 16
        rest = code - a * 49
        b = (rest * 9363) >> 16
        dz = rest - b * 7
        near_x = jnp.clip(x + a - 3, 0, 7)
        near_y = jnp.clip(y + b - 3, 0, 7)
        near_z = jnp.clip(z + dz - 3, 0, LANES - 1)
        near = near_x * 8 + near_y
        index = (near + (dz & 1) * ROWS, near + (1 - (dz & 1)) * ROWS)
        own = cell >> 7
        centre = (own + ROWS, own)
        d = dz >> 1
        low, first, third = d < 2, d < 1, d < 3
        left = lane_step < ROWS
        both, third_of, colour_of = [], [], []
        for k in range(4):
            at = slice(k * size, (k + 1) * size)
            even = [window[0, at, p * LANES : (p + 1) * LANES] for p in range(2)]
            odd = [window[1, at, p * LANES : (p + 1) * LANES] for p in range(2)] if k < 3 else even
            x_whole = jnp.where(left, even[0], odd[0]).astype(jnp.int32)
            y_whole = jnp.where(left, even[1], odd[1]).astype(jnp.int32)
            both.append((x_whole << 16) | y_whole)
            third_of.append(jnp.where(left, odd[0], even[0]))
            colour_of.append(jnp.where(left, odd[1], even[1]))

        def pick(tabs, swapped):
            got = [lane_take(t, index[swapped]) for t in tabs]
            value = jnp.where(
                low, jnp.where(first, got[0], got[1]), jnp.where(third, got[2], got[3])
            )
            return value, lane_take(tabs[1], centre[swapped])

        at_near, at_own = pick(both, 0)
        z_near, z_own = pick(third_of, 1)
        c_near, c_own = pick(colour_of, 1)
        diff = (
            ((at_near >> 16) - (at_own >> 16)).astype(jnp.float32) * (1.0 / SCALE),
            ((at_near & 65535) - (at_own & 65535)).astype(jnp.float32) * (1.0 / SCALE),
            z_near - z_own,
            c_near - c_own,
        )
        ox = (near_x - x).astype(jnp.float32) + diff[0]
        oy = (near_y - y).astype(jnp.float32) + diff[1]
        oz = (near_z - z).astype(jnp.float32) + diff[2]
        w = diff[3] * jnp.exp(-(ox * ox + oy * oy + oz * oz) / SMOOTH_SQ)
        wx, wy, wz = w * ox, w * oy, w * oz
        terms = (w, wx, wy, wz, wx * ox, wy * oy, wz * oz, wx * oy, wx * oz, wy * oz)
        return [jnp.sum(term, axis=1, keepdims=True) for term in terms]

    slot = lax.broadcasted_iota(jnp.int32, (size, 1), 0)
    kappa = jnp.where(slot < count, final_curvature(*group()), 0.0)

    sub = lax.broadcasted_iota(jnp.int32, (ROWS, width), 0)
    row_hot = jnp.where(sub == (row[0:1, :width] >> 7), 1.0, 0.0).astype(jnp.bfloat16)[:, :size]
    spread = jnp.where(lane_step == (place[0:size, :] & 127), SIGMA * kappa, 0.0)
    parts = jnp.dot(
        row_hot, jnp.concatenate(pieces(spread), axis=1), preferred_element_type=jnp.float32
    )
    added[...] = parts[:, :LANES] + parts[:, LANES : 2 * LANES] + parts[:, 2 * LANES :]

    moments[0:size, :] = jnp.broadcast_to(kappa, (size, LANES))
    moments[size:width, :] = jnp.zeros((width - size, LANES), jnp.float32)
    turned = [moments[at : at + LANES, :].T[0:1] for at in range(0, width, LANES)]
    turned = jnp.concatenate(turned + [jnp.zeros((1, 2 * LANES), jnp.float32)], axis=1)
    kappa_ref[0] = turned[:, :SLOTS]


def curvature_kernel(
    jitter_hbm, colour_hbm, cells_hbm, codes_hbm, counts_ref, source_hbm, pressure_hbm,
    kappa_ref, own_ref, rhs_ref, even_ref, odd_ref,
    jitter_ref, colour_ref, cells_ref, codes_ref, source_ref, arrived,
    table, hot, window, place, row, moments, added,
):
    copies = [
        pltpu.make_async_copy(source, target, arrived.at[i])
        for i, (source, target) in enumerate((
            (cells_hbm, cells_ref),
            (jitter_hbm, jitter_ref),
            (colour_hbm, colour_ref),
            (codes_hbm, codes_ref),
            (source_hbm, source_ref),
            (pressure_hbm, own_ref),
        ))
    ]
    for copy in copies:
        copy.start()

    copies[0].wait()
    row[...] = jnp.zeros_like(row)
    row[0:1, 0:SLOTS] = cells_ref[0]
    cells_row = row[0:1, :]
    as_float = cells_row.astype(jnp.float32)
    for h in range(2):
        part = jnp.broadcast_to(as_float[:, h * LANES : (h + 1) * LANES], (LANES, LANES))
        turned = part.T.astype(jnp.int32)
        keep = min(LANES, SLOTS - h * LANES)
        place[h * LANES : h * LANES + keep, :] = turned[:keep]

    lane = lax.broadcasted_iota(jnp.int32, (SLOTS, LANES), 1)
    z_of = place[...] & 127
    for step in range(7):
        target = jnp.clip(z_of + (step - 3), 0, LANES - 1)
        one = jnp.where(lane == target, 1.0, 0.0).astype(jnp.bfloat16)
        for q in range(3):
            hot[step % 2, (step // 2) * SLOTS : (step // 2 + 1) * SLOTS, q * LANES : (q + 1) * LANES] = one

    for copy in copies[1:]:
        copy.wait()
    whole_x = jnp.round(jitter_ref[0] * SCALE)
    whole_y = jnp.round(jitter_ref[1] * SCALE) + 32768.0
    for c, value in enumerate((whole_x, jitter_ref[2], whole_y, colour_ref[...])):
        for q, piece in enumerate(pieces(value.reshape(ROWS, LANES))):
            columns = slice(q * LANES, (q + 1) * LANES)
            table[0, c * ROWS : (c + 1) * ROWS, columns] = piece
            table[1, (c ^ 1) * ROWS : ((c ^ 1) + 1) * ROWS, columns] = piece

    count = counts_ref[0, 0]
    rest = (codes_ref, kappa_ref, table, hot, window, place, row, moments, added)
    pl.when(count <= SIZES[0])(lambda: curvature_of(SIZES[0], count, *rest))
    pl.when((count > SIZES[0]) & (count <= SIZES[1]))(lambda: curvature_of(SIZES[1], count, *rest))
    pl.when(count > SIZES[1])(lambda: curvature_of(SLOTS, count, *rest))

    rhs = source_ref[...] + added[...].reshape(8, 8, LANES)
    rhs_ref[...] = rhs
    even = lax.rem(lax.axis_index("gx"), 2) == 0
    pressure = own_ref[...]

    def send(ref, high):
        ref[0:3] = jnp.where(high, pressure[5:8], pressure[0:3])
        ref[3:5] = jnp.where(high, rhs[6:8], rhs[0:2])

    send(even_ref, even)
    send(odd_ref, jnp.logical_not(even))


def curvature_call(*values):
    tile = jax.ShapeDtypeStruct((8, 8, LANES), jnp.float32)
    slab = jax.ShapeDtypeStruct((5, 8, LANES), jnp.float32)
    vmem = pl.BlockSpec(memory_space=pltpu.VMEM)
    hbm = pl.BlockSpec(memory_space=pltpu.HBM)
    smem = pl.BlockSpec(memory_space=pltpu.SMEM)
    return pl.pallas_call(
        curvature_kernel,
        out_shape=(jax.ShapeDtypeStruct((1, 1, SLOTS), jnp.float32), tile, tile, slab, slab),
        in_specs=[hbm] * 4 + [smem] + [hbm] * 2,
        out_specs=(vmem,) * 5,
        scratch_shapes=[
            pltpu.VMEM((3, 8, 8, LANES), jnp.float32),
            pltpu.VMEM((8, 8, LANES), jnp.float32),
            pltpu.VMEM((1, 1, SLOTS), jnp.int32),
            pltpu.VMEM((1, 1, SLOTS, LANES), jnp.int32),
            pltpu.VMEM((8, 8, LANES), jnp.float32),
            pltpu.SemaphoreType.DMA((6,)),
            pltpu.VMEM((2, 4 * ROWS, 3 * LANES), jnp.bfloat16),
            pltpu.VMEM((2, 4 * SLOTS, 3 * LANES), jnp.bfloat16),
            pltpu.VMEM((2, 4 * SLOTS, 4 * ROWS), jnp.float32),
            pltpu.VMEM((SLOTS, LANES), jnp.int32),
            pltpu.VMEM((8, 2 * LANES), jnp.int32),
            pltpu.VMEM((2 * LANES, LANES), jnp.float32),
            pltpu.VMEM((ROWS, LANES), jnp.float32),
        ],
        compiler_params=pltpu.CompilerParams(vmem_limit_bytes=16 * 2**20),
        name="curvature",
    )(*values)


def sides(first, second, even):
    return jnp.where(even, second, first), jnp.where(even, first, second)


CORNERS = (
    (False, 1, 0), (False, 2, 0), (False, 2, 1), (False, 4, 0),
    (True, 0, 0), (True, 0, 1), (True, 3, 0), (True, 1, 0),
)


def edges_kernel(pressure_ref, rhs_ref, xe_ref, xo_ref, even_ref, odd_ref):
    odd_x = lax.rem(lax.axis_index("gx"), 2)
    even_y = lax.rem(lax.axis_index("gy"), 2) == 0

    def send(tile, rows, high, low):
        even_ref[tile, rows] = jnp.where(even_y, high, low)
        odd_ref[tile, rows] = jnp.where(even_y, low, high)

    for tile in range(5):
        ref, away = (pressure_ref, tile) if tile < 3 else (rhs_ref, tile - 3)
        send(tile, slice(0, 8), ref[:, 7 - away, :], ref[:, away, :])
    for at, (above, tile, away) in enumerate(CORNERS):
        ends = []
        for row in (7 - away, away):
            pair = (xe_ref[1 - odd_x, tile, row : row + 1, :], xo_ref[tile, row : row + 1, :])
            ends.append(sides(*pair, odd_x == 0)[int(above)])
        send(5, slice(at, at + 1), *ends)


def edges_call(pressure, rhs, xe, xo):
    vmem = pl.BlockSpec(memory_space=pltpu.VMEM)
    strip = jax.ShapeDtypeStruct((6, 8, LANES), jnp.float32)
    return pl.pallas_call(
        edges_kernel,
        out_shape=(strip, strip),
        in_specs=[vmem] * 4,
        out_specs=(vmem, vmem),
        compiler_params=pltpu.CompilerParams(vmem_limit_bytes=8 * 2**20),
        name="edges",
    )(pressure, rhs, xe, xo)


def sweeps_kernel(
    n_gx, n_gy, kappa_ref, pressure_ref, rhs_ref, xe_ref, xo_ref, ye_ref, yo_ref,
    out_ref, curvature_ref, wide, source,
):
    at_x, at_y = lax.axis_index("gx"), lax.axis_index("gy")
    odd_x, odd_y = lax.rem(at_x, 2), lax.rem(at_y, 2)
    below, above = sides(xe_ref[1 - odd_x], xo_ref[...], odd_x == 0)
    paired = (at_y > 0) & (at_y < n_gy - 1)
    left, right = sides(ye_ref[...], jnp.where(paired, yo_ref[odd_y], 0.0), odd_y == 0)
    curvature_ref[...] = kappa_ref[...]
    wide[:, 8:, :] = jnp.zeros((14, 8, LANES), jnp.float32)
    source[:, 8:, :] = jnp.zeros((12, 8, LANES), jnp.float32)
    wide[0:3, 0:8, :], wide[3:11, 0:8, :], wide[11:14, 0:8, :] = below[0:3], pressure_ref[...], above[0:3]
    source[0:2, 0:8, :], source[2:10, 0:8, :], source[10:12, 0:8, :] = below[3:5], rhs_ref[...], above[3:5]
    for part, rows in ((right, (8, 9, 10)), (left, (15, 14, 13))):
        for tile in range(3):
            wide[3:11, rows[tile], :] = part[tile]
        for tile in range(2):
            source[2:10, rows[tile], :] = part[3 + tile]
        for at, (high, tile, away) in enumerate(CORNERS):
            row = rows[away]
            if tile < 3:
                plane = 11 + tile if high else tile
                wide[plane, row : row + 1, :] = part[5, at : at + 1]
            else:
                plane = 10 + tile - 3 if high else tile - 3
                source[plane, row : row + 1, :] = part[5, at : at + 1]
    current, rhs = wide[...], source[...]
    lane = lax.broadcasted_iota(jnp.int32, (1, 16, LANES), 2)
    sub = lax.broadcasted_iota(jnp.int32, (1, 16, LANES), 1)
    inside = (sub < jnp.where(at_y < n_gy - 1, 12, 8)) | (sub >= jnp.where(at_y > 0, 12, 16))
    for sweep in range(3):
        mid = current[1:-1]
        beside = current[2:] + current[:-2]
        beside = beside + pltpu.roll(mid, 15, 1) + pltpu.roll(mid, 1, 1)
        beside = beside + jnp.where(lane < LANES - 1, pltpu.roll(mid, LANES - 1, 2), 0.0)
        beside = beside + jnp.where(lane > 0, pltpu.roll(mid, 1, 2), 0.0)
        current = (beside + rhs[sweep : 12 - sweep]) / 6.0
        if sweep < 2:
            count = 12 - 2 * sweep
            plane = lax.broadcasted_iota(jnp.int32, (count, 1, 1), 0) + (sweep - 2)
            held = (plane >= jnp.where(at_x > 0, -2, 0)) & (plane < jnp.where(at_x < n_gx - 1, 10, 8))
            current = jnp.where(held & inside, current, 0.0)
    out_ref[...] = current[:, 0:8, :]


def sweeps_call(n_gx, n_gy, *values):
    vmem = pl.BlockSpec(memory_space=pltpu.VMEM)
    return pl.pallas_call(
        functools.partial(sweeps_kernel, n_gx, n_gy),
        out_shape=(
            jax.ShapeDtypeStruct((8, 8, LANES), jnp.float32),
            jax.ShapeDtypeStruct((1, 1, SLOTS), jnp.float32),
        ),
        in_specs=[vmem] * 7,
        out_specs=(vmem, vmem),
        scratch_shapes=[
            pltpu.VMEM((14, 16, LANES), jnp.float32),
            pltpu.VMEM((12, 16, LANES), jnp.float32),
        ],
        compiler_params=pltpu.CompilerParams(vmem_limit_bytes=8 * 2**20),
        name="sweeps",
    )(*values)


def swap_odd(value, axis):
    pairs = []
    for i in range(1, lax.axis_size(axis) - 1, 2):
        pairs += [(i, i + 1), (i + 1, i)]
    return lax.ppermute(value, axis, pairs)


def gather_even(value, axis):
    groups = [[i, i + 1] for i in range(0, lax.axis_size(axis), 2)]
    return lax.all_gather(value, axis, axis=0, axis_index_groups=groups)


def swap_even(value, axis):
    pairs = []
    for i in range(0, lax.axis_size(axis), 2):
        pairs += [(i, i + 1), (i + 1, i)]
    return lax.ppermute(value, axis, pairs)


def gather_odd(value, outer, axis):
    rows, size = lax.axis_size(outer), lax.axis_size(axis)
    groups = [[i * size + j, i * size + j + 1] for i in range(rows) for j in range(1, size - 1, 2)]
    groups += [[i * size + j, (i + 1) * size + j] for i in range(0, rows, 2) for j in (0, size - 1)]
    return lax.all_gather(value, (outer, axis), axis=0, axis_index_groups=groups)


def held(value):
    return pltpu.with_memory_space_constraint(value, pltpu.HBM)


def per_device(jitter, colour, surface_cells, neighbours, counts, pressure, source):
    kappa, own, rhs, even, odd = curvature_call(
        held(jitter), held(colour), held(surface_cells), held(neighbours),
        counts, held(source), held(pressure),
    )
    xo, xe = swap_odd(odd, "gx"), gather_even(even, "gx")
    even, odd = edges_call(own, rhs, xe, xo)
    ye, yo = swap_even(even, "gy"), gather_odd(odd, "gx", "gy")
    return sweeps_call(
        lax.axis_size("gx"), lax.axis_size("gy"), kappa, own, rhs, xe, xo, ye, yo
    )


def solution(mesh):
    placed = (
        P(None, "gx", "gy", None),
        P("gx", "gy", None),
        P("gx", "gy", None),
        P("gx", "gy", None, None),
        P("gx", "gy"),
        P("gx", "gy", None),
        P("gx", "gy", None),
    )
    return jax.shard_map(
        per_device,
        mesh=mesh,
        in_specs=placed,
        out_specs=(P("gx", "gy", None), P("gx", "gy", None)),
        check_vma=False,
    )
```
